128 devices in a mesh: dp: 16 (over x, z), fsdp: 8 (over y, core).
Axes of the slice: x: 4, y: 4, z: 4, core: 2. Of those that a mesh axis runs over, the one named last changes fastest.
Arguments:
- points: bfloat16 [262144, 512], P(('dp', 'fsdp')), may hold values from -8 to 8
- cotangent: bfloat16 [262144, 512], P(('dp', 'fsdp')), may hold values from -6 to 6
- destination: int32 [262144], P(('dp', 'fsdp')), may hold values from 0 to 127, as said below
- curve_slot: int32 [262144], P(('dp', 'fsdp')), may hold values from 0 to 1023, as said below
- point_counts: int32 [128], P(('dp', 'fsdp')), may hold values from 0 to 2048, as said below
- shift_offset: int32 [1], replicated, may hold values from 1 to 1023
- project_in: bfloat16 [512, 1536], P('fsdp'), may hold values from -8 to 8
- project_out: bfloat16 [512, 512], P('fsdp'), may hold values from -0.5 to 0.5
- norm_gain: bfloat16 [512], P('fsdp'), may hold values from 0.099609375 to 1.8984375
Outputs:
- block_out: bfloat16 [262144, 512], P(('dp', 'fsdp'))
- point_grad: bfloat16 [262144, 512], P(('dp', 'fsdp'))
- grad_in: float32 [512, 1536], P('fsdp')
- grad_out: float32 [512, 512], P('fsdp')
- grad_gain: float32 [512], P('fsdp')
The draws below stay inside these ranges and needn't reach their ends.
Inputs may be any that keep to these rules, and one draw needn't show every extreme that they name: Rows at or past their device's count carry no meaning. Among the counting rows of one device at most 16 name one destination, and some device sends exactly 16 to every destination. Over the counting rows of all devices every pair of destination and curve_slot occurs exactly once. `point_counts`: they sum to 131072; some device holds exactly 2048.
All inputs are finite; a program needn't handle non-finite values.
Results may differ from the reference program's by a relative error of at most 0.006.
The reference program's roundings to bfloat16 on the way count: a program that leaves them out, or rounds other values in their place, can miss the bound.
Values may be sent and summed in bfloat16 or wider, within the bound.
No kernel may reach another device: no remote copies, remote signals or barrier semaphores. Data moves between devices by JAX's collectives and lax.ppermute only.
A program may use at most 128 MiB of HBM per device.

```python
import math
import jax
import jax.numpy as jnp
from jax import lax

D = 512
HEADS = 16
PATCH = 1024
ROWS = 1024
CAP = 16
ACQ = 2048
TOTAL = 131072
INPUT_ROWS = 262144


def routing_tables(key):
    devices = ACQ // CAP
    half = CAP // 2
    pairs = devices // 2
    keys = jax.random.split(key, 5)
    swing = jax.random.randint(keys[0], (pairs,), -(half // 2), half // 2 + 1)
    chosen = jax.random.randint(keys[1], (), 0, pairs)
    swing = jnp.where(jnp.arange(pairs) == chosen, half, swing)
    loads = jnp.stack([half + swing, half - swing], axis=1).reshape(devices)
    room = half - jnp.abs(swing) + 1
    tilt = jnp.repeat(jax.random.randint(keys[2], (pairs,), 0, 1 << 20) % room, 2)
    source = jnp.arange(devices)
    parity = 1 - 2 * ((source[:, None] + source[None, :]) % 2)
    table = loads[:, None] + tilt[:, None] * parity
    counts = jnp.sum(table, axis=1).astype(jnp.int32)
    starts = jnp.cumsum(table, axis=0) - table
    candidate = jnp.arange(ACQ)
    cand_dest = candidate // CAP
    cand_rank = candidate % CAP

    def arrange(row_key, row_table, row_starts):
        used = (cand_rank < row_table[cand_dest]).astype(jnp.int32)
        scores = (1 - used) * ACQ + jax.random.permutation(row_key, ACQ)
        picked = jnp.argsort(scores, stable=True)
        return (picked // CAP, picked % CAP, row_starts[picked // CAP])
    dest, rank, base = jax.vmap(arrange)(jax.random.split(keys[3], devices), table, starts)

    def shuffle(row_key):
        return jax.random.permutation(row_key, ROWS)
    orders = jax.vmap(shuffle)(jax.random.split(keys[4], devices))
    slot = orders[dest, (base + rank) % ROWS]
    return (dest.reshape(-1).astype(jnp.int32), slot.reshape(-1).astype(jnp.int32), counts)


def draw_destination(key, part):
    return routing_tables(key)[0]


def draw_curve_slot(key, part):
    return routing_tables(key)[1]


def draw_point_counts(key, part):
    return routing_tables(key)[2]


def draw_points(key, part):
    key = jax.random.fold_in(key, 5)
    keys = jax.random.split(key, 1)
    values = jnp.clip(jax.random.normal(keys[0], (INPUT_ROWS, D), jnp.float32), -6.0, 6.0)
    return values.astype(jnp.bfloat16)


def draw_project_in(key, part):
    key = jax.random.fold_in(key, 7)
    spread = math.sqrt(2.0 / D)
    values = jnp.clip(jax.random.normal(key, (D, 3 * D), jnp.float32), -6.0, 6.0) * spread
    return values.astype(jnp.bfloat16)


def level_of(stream_key, shape, cuts, least, high):
    def one(dim, parts):
        heights = jax.random.uniform(jax.random.fold_in(jax.random.fold_in(stream_key, 6), dim), (parts,), jnp.float32, least / len(cuts), high / len(cuts))
        return jnp.repeat(jnp.exp(heights), shape[dim] // parts).reshape((-1,) + (1,) * (len(shape) - dim - 1))

    level = one(*cuts[0])
    for cut in cuts[1:]:
        level = level * one(*cut)
    return level


def bell_draw(rng, dims, deviation, most, pieces=(), kind=jnp.bfloat16):
    factor_of = level_of(rng, dims, pieces, -0.22, 0.18) if pieces else 1.0
    drawn = jax.random.normal(rng, dims, jnp.float32) * deviation * factor_of
    return jnp.minimum(jnp.maximum(drawn, -most), most).astype(kind)


def setup_inputs(seed: int = 0) -> dict:
    key_of = jax.random.split(jax.random.key(seed), 10)
    return {
        "points": draw_points(jax.random.fold_in(key_of[9], 71), 0),
        "cotangent": bell_draw(key_of[1], (INPUT_ROWS, D), 1.0, 6.0, ((0, 128),)),
        "destination": draw_destination(jax.random.fold_in(key_of[9], 71), 0),
        "curve_slot": draw_curve_slot(jax.random.fold_in(key_of[9], 71), 0),
        "point_counts": draw_point_counts(jax.random.fold_in(key_of[9], 71), 0),
        "shift_offset": jax.random.randint(key_of[5], (1,), 1, PATCH).astype(jnp.int32),
        "project_in": draw_project_in(jax.random.fold_in(key_of[9], 71), 0),
        "project_out": bell_draw(key_of[7], (D, D), (D // 4) ** -0.5, 0.5, ((0, 8),)),
        "norm_gain": jnp.clip(1.0 + 0.18 * jax.random.normal(key_of[8], (D,), jnp.float32), 0.099609375, 1.8984375).astype(jnp.bfloat16),
    }


EPS = 1e-05

def layer_stats(values_in):
    values = values_in.astype(jnp.float32)
    center = values - lax.optimization_barrier(jnp.mean(values, axis=-1, keepdims=True))
    inverse = lax.rsqrt(lax.optimization_barrier(jnp.mean(center * center, axis=-1, keepdims=True)) + EPS)
    return (center * inverse, inverse)

def split_heads(block, heads):
    length = block.shape[0]
    head_width = block.shape[1] // heads
    group = math.gcd(heads, 4)
    shaped = block.reshape(length, heads // group, group, head_width)
    return jnp.transpose(shaped, (1, 0, 2, 3))

def join_heads(items):
    length = items.shape[1]
    return jnp.transpose(items, (1, 0, 2, 3)).reshape(length, -1)

def probabilities(query, keys, keep):
    scale = query.shape[-1] ** (-0.5)
    scores = jnp.einsum('qhe,khe->hqk', query.astype(jnp.float32), keys.astype(jnp.float32)) * scale
    scores = jnp.where(keep[None, None, :], scores, -1e+30)
    top = lax.optimization_barrier(jnp.max(scores, axis=-1, keepdims=True))
    weights = jnp.exp(scores - top)
    return weights / lax.optimization_barrier(jnp.sum(weights, axis=-1, keepdims=True))

def patch_pass(project_in, project_out, norm_gain, rows_in, cot_rows, keep):
    width = rows_in.shape[1]
    heads = HEADS
    normed, inv_std = layer_stats(rows_in)
    gain = norm_gain.astype(jnp.float32)
    hidden = (normed * gain).astype(jnp.bfloat16)
    projected = jnp.dot(hidden, project_in, preferred_element_type=jnp.float32).astype(jnp.bfloat16)
    queries = split_heads(projected[:, :width], heads)
    keyset = split_heads(projected[:, width:2 * width], heads)
    valueset = split_heads(projected[:, 2 * width:], heads)

    def forward_item(item):
        query, keys, values = item
        probs_b = probabilities(query, keys, keep).astype(jnp.bfloat16)
        return jnp.einsum('hqk,khe->qhe', probs_b.astype(jnp.float32), values.astype(jnp.float32)).astype(jnp.bfloat16)
    att_items = lax.map(forward_item, (queries, keyset, valueset))
    attended = join_heads(att_items)
    block = (rows_in.astype(jnp.float32) + jnp.dot(attended, project_out, preferred_element_type=jnp.float32)).astype(jnp.bfloat16)
    grad_att = lax.dot_general(cot_rows, project_out, (((1,), (1,)), ((), ())), preferred_element_type=jnp.float32).astype(jnp.bfloat16)
    grad_items = split_heads(grad_att, heads)

    def backward_item(item):
        query, keys, values, output, upstream = item
        scale = query.shape[-1] ** (-0.5)
        probs = probabilities(query, keys, keep)
        probs_b = probs.astype(jnp.bfloat16)
        upstream_f = upstream.astype(jnp.float32)
        along = jnp.einsum('qhe,khe->hqk', upstream_f, values.astype(jnp.float32))
        offset = lax.optimization_barrier(jnp.sum(upstream_f * output.astype(jnp.float32), axis=-1))
        slopes = (probs * (along - jnp.transpose(offset)[:, :, None]) * scale).astype(jnp.bfloat16)
        slopes_f = slopes.astype(jnp.float32)
        query_grad = jnp.einsum('hqk,khe->qhe', slopes_f, keys.astype(jnp.float32))
        key_grad = jnp.einsum('hqk,qhe->khe', slopes_f, query.astype(jnp.float32))
        value_grad = jnp.einsum('hqk,qhe->khe', probs_b.astype(jnp.float32), upstream_f)
        return (query_grad, key_grad, value_grad)
    query_grad, key_grad, value_grad = lax.map(backward_item, (queries, keyset, valueset, att_items, grad_items))
    grad_rows = jnp.concatenate([join_heads(query_grad), join_heads(key_grad), join_heads(value_grad)], axis=1).astype(jnp.bfloat16)
    grad_hidden = lax.dot_general(grad_rows, project_in, (((1,), (1,)), ((), ())), preferred_element_type=jnp.float32)
    part_in = lax.dot_general(hidden, grad_rows, (((0,), (0,)), ((), ())), preferred_element_type=jnp.float32)
    part_out = lax.dot_general(attended, cot_rows, (((0,), (0,)), ((), ())), preferred_element_type=jnp.float32)
    part_gain = lax.optimization_barrier(jnp.sum(grad_hidden * normed, axis=0))
    scaled = grad_hidden * gain
    curve_grad = cot_rows.astype(jnp.float32) + inv_std * (scaled - lax.optimization_barrier(jnp.mean(scaled, axis=-1, keepdims=True)) - normed * lax.optimization_barrier(jnp.mean(scaled * normed, axis=-1, keepdims=True)))
    return (block, curve_grad.astype(jnp.bfloat16), part_in, part_out, part_gain)

def reference(points, cotangent, destination, curve_slot, point_counts, shift_offset, project_in, project_out, norm_gain):
    width = points.shape[1]
    position = jnp.arange(INPUT_ROWS, dtype=jnp.int32)
    counting = position % ACQ < point_counts[position // ACQ]
    place = jnp.where(counting, destination * ROWS + curve_slot, TOTAL).astype(jnp.int32)
    curve_points = jnp.zeros((TOTAL, width), jnp.bfloat16).at[place].set(points, mode='drop')
    curve_cot = jnp.zeros((TOTAL, width), jnp.bfloat16).at[place].set(cotangent, mode='drop')
    front = (PATCH - shift_offset[0]).astype(jnp.int32)
    padded_len = TOTAL + PATCH
    start = (front, jnp.zeros((), jnp.int32))
    padded_points = lax.dynamic_update_slice(jnp.zeros((padded_len, width), jnp.bfloat16), curve_points, start)
    padded_cot = lax.dynamic_update_slice(jnp.zeros((padded_len, width), jnp.bfloat16), curve_cot, start)
    index = jnp.arange(padded_len, dtype=jnp.int32)
    keep = (index >= front) & (index < front + TOTAL)
    count_blocks = padded_len // PATCH

    def step(carry, inputs):
        rows_in, cot_rows, keep_rows = inputs
        block, grad_block, part_in, part_out, part_gain = patch_pass(project_in, project_out, norm_gain, rows_in, cot_rows, keep_rows)
        return ((carry[0] + part_in, carry[1] + part_out, carry[2] + part_gain), (block, grad_block))
    initial = (jnp.zeros((width, 3 * width), jnp.float32), jnp.zeros((width, width), jnp.float32), jnp.zeros((width,), jnp.float32))
    sums, outputs = lax.scan(step, initial, (padded_points.reshape(count_blocks, PATCH, width), padded_cot.reshape(count_blocks, PATCH, width), keep.reshape(count_blocks, PATCH)))
    curve_out = lax.dynamic_slice(outputs[0].reshape(padded_len, width), start, (TOTAL, width))
    curve_grad = lax.dynamic_slice(outputs[1].reshape(padded_len, width), start, (TOTAL, width))
    safe = jnp.minimum(place, TOTAL - 1)
    block_out = jnp.where(counting[:, None], curve_out[safe], jnp.zeros((), jnp.bfloat16))
    point_grad = jnp.where(counting[:, None], curve_grad[safe], jnp.zeros((), jnp.bfloat16))
    return (block_out, point_grad, sums[0], sums[1], sums[2])
```

```python
import jax
import jax.numpy as jnp
from jax import lax
from jax.experimental import pallas as pl
from jax.experimental.pallas import tpu as pltpu
from jax.sharding import PartitionSpec as P

HEADS = 16
PATCH = 1024
EPS = 1e-05
BOTH = ("dp", "fsdp")
GAIN_COLS = 128
FAR = -1e30
LOG2E = 1.4426950408889634
F32 = jnp.float32
BF16 = jnp.bfloat16
VMEM_BYTES = 60 * 1024 * 1024


def params(steps=1):
    return pltpu.CompilerParams(
        vmem_limit_bytes=VMEM_BYTES, dimension_semantics=("arbitrary",) * steps
    )


def whole(shape):
    zeros = (0,) * len(shape)
    return pl.BlockSpec(shape, lambda *_: zeros)


SMEM = pl.BlockSpec(memory_space=pltpu.SMEM)


def ones_where(mask, dtype=BF16):
    return jnp.where(mask, 1.0, 0.0).astype(dtype)


def iota(shape, dim):
    return lax.broadcasted_iota(jnp.int32, shape, dim)


def nt(a, b):
    return lax.dot_general(a, b, (((1,), (1,)), ((), ())), preferred_element_type=F32)


def nn(a, b):
    return jnp.dot(a, b, preferred_element_type=F32)


def pick_rows(index_row, rows, first, count):
    slots = index_row.shape[1]
    chosen = ones_where(iota((count, slots), 0) + first == index_row)
    return nn(chosen, rows).astype(BF16)


def send_plan(shift, count, dest_ref, slot_ref, target_ref, marks_ref):
    devices, capacity = marks_ref.shape
    arrived = dest_ref.shape[1]
    chunk = 256
    before = ones_where(iota((chunk, chunk), 0) < iota((chunk, chunk), 1))
    base = jnp.zeros((devices, 1), F32)
    marks = jnp.zeros((devices, capacity), F32)
    for start in range(0, arrived, chunk):
        cols = pl.ds(start, chunk)
        dest = dest_ref[:, cols]
        valid = iota((1, chunk), 1) + start < count
        here = jnp.where(
            (iota((devices, chunk), 0) == dest) & valid, 1.0, 0.0
        )
        ahead = nn(here.astype(BF16), before) + base
        rank = jnp.sum(here * ahead, axis=0, keepdims=True).astype(jnp.int32)
        base = base + jnp.sum(here, axis=1, keepdims=True)
        target_ref[:, cols] = jnp.where(valid, dest * capacity + rank, -1)
        code = jnp.where(slot_ref[:, cols] < shift, 2.0, 1.0)
        at_rank = ones_where(iota((capacity, chunk), 0) == rank)
        marks = marks + nt((here * code).astype(BF16), at_rank)
    marks_ref[...] = marks.astype(BF16)


def send_first_kernel(
    shift_ref, count_ref, dest_ref, slot_ref, rows_ref, send_ref, target_ref, marks_ref
):
    step = pl.program_id(0)

    @pl.when(step == 0)
    def _():
        send_plan(shift_ref[0], count_ref[0], dest_ref, slot_ref, target_ref, marks_ref)

    block = send_ref.shape[0]
    send_ref[...] = pick_rows(target_ref[...], rows_ref[...], step * block, block)


def send_first(shift, count, dest, slot, rows, devices, block=512):
    arrived, width = rows.shape
    return pl.pallas_call(
        send_first_kernel,
        grid=(arrived // block,),
        in_specs=[
            SMEM,
            SMEM,
            whole((1, arrived)),
            whole((1, arrived)),
            whole((arrived, width)),
        ],
        out_specs=[
            pl.BlockSpec((block, width), lambda i: (i, 0)),
            whole((1, arrived)),
            whole((devices, arrived // devices)),
        ],
        out_shape=[
            jax.ShapeDtypeStruct((arrived, width), BF16),
            jax.ShapeDtypeStruct((1, arrived), jnp.int32),
            jax.ShapeDtypeStruct((devices, arrived // devices), BF16),
        ],
        compiler_params=params(),
        name="send_first",
    )(shift, count, dest, slot, rows)


def pick_kernel(index_ref, rows_ref, out_ref):
    block = out_ref.shape[0]
    out_ref[...] = pick_rows(index_ref[...], rows_ref[...], pl.program_id(0) * block, block)


def pick(index, rows, out_rows, name, block=512):
    arrived, width = rows.shape
    return pl.pallas_call(
        pick_kernel,
        grid=(out_rows // block,),
        in_specs=[whole((1, arrived)), whole((arrived, width))],
        out_specs=pl.BlockSpec((block, width), lambda i: (i, 0)),
        out_shape=jax.ShapeDtypeStruct((out_rows, width), BF16),
        compiler_params=params(),
        name=name,
    )(index, rows)


def place_kernel(shift_ref, marks_ref, place_ref):
    devices, capacity = marks_ref.shape
    slots = devices * capacity
    marks = marks_ref[...].astype(F32)
    lower = ones_where(iota((devices, devices), 1) < iota((devices, devices), 0))
    before = ones_where(iota((capacity, capacity), 0) < iota((capacity, capacity), 1))
    place = jnp.full((devices, capacity), -1.0, F32)
    for code, first in ((1.0, 0), (2.0, PATCH - shift_ref[0])):
        mine = marks == code
        flags = ones_where(mine)
        earlier = jnp.sum(nn(lower, flags), axis=1, keepdims=True) + nn(flags, before)
        place = jnp.where(mine, earlier + lax.convert_element_type(first, F32), place)
    place = place.astype(jnp.int32)
    high = lax.shift_right_arithmetic(place, 5)
    low = lax.bitwise_and(place, 31)
    spread = ones_where(
        iota((capacity, slots), 0) == lax.rem(iota((capacity, slots), 1), capacity)
    )
    own = iota((devices, slots), 0) == lax.div(iota((devices, slots), 1), capacity)

    def flat(part):
        wide = nn(part.astype(F32).astype(BF16), spread)
        return jnp.sum(jnp.where(own, wide, 0.0), axis=0, keepdims=True).astype(jnp.int32)

    place_ref[...] = flat(high) * 32 + flat(low)


def place_of(shift, marks):
    devices, capacity = marks.shape
    return pl.pallas_call(
        place_kernel,
        in_specs=[SMEM, whole((devices, capacity))],
        out_specs=whole((1, devices * capacity)),
        out_shape=jax.ShapeDtypeStruct((1, devices * capacity), jnp.int32),
        compiler_params=params(0),
        grid=(),
        name="place",
    )(shift, marks)


def column_of(row):
    length = row.shape[1]
    return jnp.transpose(jnp.broadcast_to(row, (128, length)))


def spread_rows(index_row, rows):
    wide = column_of(index_row)
    count = wide.shape[0]
    lanes = iota((count, 128), 1)
    chosen = jnp.concatenate(
        [ones_where(wide == lanes + start) for start in range(0, rows.shape[0], 128)], axis=1
    )
    return nn(chosen, rows).astype(BF16)


def spread_kernel(index_ref, rows_ref, out_ref):
    out_ref[...] = spread_rows(index_ref[...], rows_ref[...])


def spread(index, rows, name, block=512):
    slots = index.shape[1]
    source, width = rows.shape
    return pl.pallas_call(
        spread_kernel,
        grid=(slots // block,),
        in_specs=[pl.BlockSpec((1, block), lambda i: (0, i)), whole((source, width))],
        out_specs=pl.BlockSpec((block, width), lambda i: (i, 0)),
        out_shape=jax.ShapeDtypeStruct((slots, width), BF16),
        compiler_params=params(),
        name=name,
    )(index, rows)


def spread_pair_kernel(shift_ref, index_ref, own_ref, back_ref, ahead_ref, out_ref, rows):
    @pl.when(pl.program_id(0) == 0)
    def _():
        rows[...] = joined(shift_ref[0], own_ref, back_ref, ahead_ref)

    out_ref[...] = spread_rows(index_ref[...], rows[...])


def spread_pair(shift, index, own, back, ahead, name, block=512):
    slots = index.shape[1]
    half, width = back.shape
    return pl.pallas_call(
        spread_pair_kernel,
        grid=(slots // block,),
        in_specs=[
            SMEM,
            pl.BlockSpec((1, block), lambda i: (0, i)),
            whole((2 * half, width)),
            whole((half, width)),
            whole((half, width)),
        ],
        out_specs=pl.BlockSpec((block, width), lambda i: (i, 0)),
        out_shape=jax.ShapeDtypeStruct((slots, width), BF16),
        scratch_shapes=[pltpu.VMEM((2 * half, width), BF16)],
        compiler_params=params(),
        name=name,
    )(shift, index, own, back, ahead)


def joined(shift, own_ref, top_ref, bottom_ref):
    half, width = top_ref.shape
    edge = PATCH - shift
    row = iota((half, width), 0)
    top = jnp.where((2 * shift > PATCH) & (row < edge), top_ref[...], own_ref[:half, :])
    bottom = jnp.where((2 * shift <= PATCH) & (row + half >= edge), bottom_ref[...], own_ref[half:, :])
    return jnp.concatenate([top, bottom], axis=0)


def forward_kernel(
    shift_ref,
    wrap_ref,
    own_ref,
    top_ref,
    bottom_ref,
    in_t_ref,
    out_t_ref,
    gain_ref,
    probs_ref,
    block_ref,
    hidden_ref,
    normed_ref,
    inverse_ref,
    queries_ref,
    keys_ref,
    values_ref,
    attended_ref,
    x_t,
    query_x,
    key_x,
):
    head = pl.program_id(0)
    heads, head_width, length = queries_ref.shape
    width = heads * head_width
    extra = query_x.shape[1] - head_width

    @pl.when(head == 0)
    def _():
        rows = joined(shift_ref[0], own_ref, top_ref, bottom_ref)
        values_in = jnp.transpose(rows.astype(F32))
        x_t[...] = values_in
        center = values_in - jnp.mean(values_in, axis=0, keepdims=True)
        inverse = lax.rsqrt(jnp.mean(center * center, axis=0, keepdims=True) + EPS)
        normed = center * inverse
        normed_ref[...] = normed
        inverse_ref[...] = inverse
        hidden = (normed * gain_ref[:, :1].astype(F32)).astype(BF16)
        hidden_ref[...] = hidden
        for part, ref in enumerate((queries_ref, keys_ref, values_ref)):
            rows_of = in_t_ref[part * width : (part + 1) * width, :]
            ref[...] = nn(rows_of, hidden).astype(BF16).reshape(heads, head_width, length)
        side = iota((extra, length), 1) >= PATCH - shift_ref[0]
        line = iota((extra, length), 0)
        query_side = jnp.where(((line == 0) & ~side) | ((line == 1) & side), 1.0, 0.0)
        key_side = jnp.where(((line == 0) & side) | ((line == 1) & ~side), FAR, 0.0)
        key_side = jnp.where(wrap_ref[0] > 0, key_side, 0.0)
        query_x[:, :head_width, :] = queries_ref[...]
        key_x[:, :head_width, :] = keys_ref[...]
        for h in range(heads):
            query_x[h, head_width:, :] = query_side.astype(BF16)
            key_x[h, head_width:, :] = key_side.astype(BF16)

    scale = head_width ** (-0.5) * LOG2E
    key_rows = jnp.transpose(key_x[head])
    query = query_x.at[head]
    value = values_ref[head]
    chunk = 256
    for start in range(0, length, chunk):
        cols = pl.ds(start, chunk)
        scores = nn(key_rows, query[:, cols])
        top = jnp.max(scores, axis=0, keepdims=True)
        weights = jnp.exp2((scores - top) * scale)
        probs = weights * (1.0 / jnp.sum(weights, axis=0, keepdims=True))
        probs_ref[0, :, cols] = probs
        attended_ref[head, :, cols] = nn(value, probs.astype(BF16)).astype(BF16)

    @pl.when(head == heads - 1)
    def _():
        attended = attended_ref[...].reshape(width, length)
        block = x_t[...] + nn(out_t_ref[...], attended)
        block_ref[...] = jnp.transpose(block).astype(BF16)


def forward(shift, wrap, own, top, bottom, weights, weights_t):
    length, width = own.shape
    head_width = width // HEADS
    half = length // 2
    split = jax.ShapeDtypeStruct((HEADS, head_width, length), BF16)
    return pl.pallas_call(
        forward_kernel,
        grid=(HEADS,),
        in_specs=[
            SMEM,
            SMEM,
            whole((length, width)),
            whole((half, width)),
            whole((half, width)),
            pl.BlockSpec((3 * width, width), lambda h: (0, 0)),
            pl.BlockSpec((width, width), lambda h: (3, 0)),
            pl.BlockSpec((width, GAIN_COLS), lambda h: (0, 4 * width // GAIN_COLS)),
        ],
        out_specs=[
            pl.BlockSpec((1, length, length), lambda h: (h, 0, 0)),
            whole((length, width)),
            whole((width, length)),
            whole((width, length)),
            whole((1, length)),
            whole((HEADS, head_width, length)),
            whole((HEADS, head_width, length)),
            whole((HEADS, head_width, length)),
            whole((HEADS, head_width, length)),
        ],
        out_shape=[
            jax.ShapeDtypeStruct((HEADS, length, length), F32),
            jax.ShapeDtypeStruct((length, width), BF16),
            jax.ShapeDtypeStruct((width, length), BF16),
            jax.ShapeDtypeStruct((width, length), F32),
            jax.ShapeDtypeStruct((1, length), F32),
            split,
            split,
            split,
            split,
        ],
        scratch_shapes=[
            pltpu.VMEM((width, length), F32),
            pltpu.VMEM((HEADS, head_width + 16, length), BF16),
            pltpu.VMEM((HEADS, head_width + 16, length), BF16),
        ],
        compiler_params=params(),
        name="forward",
    )(shift, wrap, own, top, bottom, weights_t, weights_t, weights)


def backward_kernel(
    shift_ref,
    own_ref,
    top_ref,
    bottom_ref,
    in_ref,
    out_ref,
    gain_ref,
    probs_ref,
    hidden_ref,
    normed_ref,
    inverse_ref,
    queries_ref,
    keys_ref,
    values_ref,
    attended_ref,
    grad_ref,
    parts_ref,
    cot,
    grad_att,
    grad_rows,
):
    head = pl.program_id(0)
    heads, head_width, length = queries_ref.shape
    width = heads * head_width

    @pl.when(head == 0)
    def _():
        rows = joined(shift_ref[0], own_ref, top_ref, bottom_ref)
        cot[...] = rows
        grad_att[...] = nt(out_ref[...], rows).astype(BF16).reshape(heads, head_width, length)

    scale = head_width ** (-0.5)
    query, key, value = queries_ref[head], keys_ref[head], values_ref[head]
    value_rows = jnp.transpose(value)
    upstream = grad_att[head]
    offset = jnp.sum(upstream.astype(F32) * attended_ref[head].astype(F32), axis=0, keepdims=True)
    chunk = 256
    key_grad = jnp.zeros((head_width, length), F32)
    value_grad = jnp.zeros((head_width, length), F32)
    for start in range(0, length, chunk):
        cols = pl.ds(start, chunk)
        probs = probs_ref[0, :, cols]
        along = nn(value_rows, upstream[:, start : start + chunk])
        slopes = (probs * (along - offset[:, start : start + chunk]) * scale).astype(BF16)
        grad_rows[0, head, :, cols] = nn(key, slopes).astype(BF16)
        key_grad = key_grad + nt(query[:, start : start + chunk], slopes)
        value_grad = value_grad + nt(upstream[:, start : start + chunk], probs.astype(BF16))
    grad_rows[1, head] = key_grad.astype(BF16)
    grad_rows[2, head] = value_grad.astype(BF16)

    @pl.when(head == heads - 1)
    def _():
        grads = grad_rows[...].reshape(3 * width, length)
        normed = normed_ref[...]
        grad_hidden = nn(in_ref[...], grads)
        parts_ref[:, : 3 * width] = nt(hidden_ref[...], grads)
        parts_ref[:, 3 * width : 4 * width] = nn(
            attended_ref[...].reshape(width, length), cot[...]
        )
        part_gain = jnp.sum(grad_hidden * normed, axis=1, keepdims=True)
        parts_ref[:, 4 * width :] = jnp.broadcast_to(part_gain, (width, GAIN_COLS))
        scaled = grad_hidden * gain_ref[:, :1].astype(F32)
        middle = jnp.mean(scaled, axis=0, keepdims=True)
        slope = jnp.mean(scaled * normed, axis=0, keepdims=True)
        change = inverse_ref[...] * (scaled - middle - normed * slope)
        grad_ref[...] = (cot[...].astype(F32) + jnp.transpose(change)).astype(BF16)


def backward(shift, own, top, bottom, weights, saved):
    length, width = own.shape
    head_width = width // HEADS
    half = length // 2
    split = (HEADS, head_width, length)
    return pl.pallas_call(
        backward_kernel,
        grid=(HEADS,),
        in_specs=[
            SMEM,
            whole((length, width)),
            whole((half, width)),
            whole((half, width)),
            pl.BlockSpec((width, 3 * width), lambda h: (0, 0)),
            pl.BlockSpec((width, width), lambda h: (0, 3)),
            pl.BlockSpec((width, GAIN_COLS), lambda h: (0, 4 * width // GAIN_COLS)),
            pl.BlockSpec((1, length, length), lambda h: (h, 0, 0)),
            whole((width, length)),
            whole((width, length)),
            whole((1, length)),
            whole(split),
            whole(split),
            whole(split),
            whole(split),
        ],
        out_specs=[whole((length, width)), whole((width, 4 * width + GAIN_COLS))],
        out_shape=[
            jax.ShapeDtypeStruct((length, width), BF16),
            jax.ShapeDtypeStruct((width, 4 * width + GAIN_COLS), F32),
        ],
        scratch_shapes=[
            pltpu.VMEM((length, width), BF16),
            pltpu.VMEM(split, BF16),
            pltpu.VMEM((3,) + split, BF16),
        ],
        compiler_params=params(),
        name="backward",
    )(shift, own, top, bottom, weights, weights, weights, *saved)


def exchange(rows, devices):
    moved = lax.all_to_all(
        rows.reshape(devices, rows.shape[0] // devices, rows.shape[1]),
        BOTH,
        split_axis=0,
        concat_axis=0,
        tiled=True,
    )
    return moved.reshape(rows.shape)


def neighbours(rows, devices):
    half = rows.shape[0] // 2
    onward = [(i, (i + 1) % devices) for i in range(devices)]
    back = [((i + 1) % devices, i) for i in range(devices)]
    return lax.ppermute(rows[:half], BOTH, onward), lax.ppermute(rows[half:], BOTH, back)


def neighbours_back(rows, devices):
    half = rows.shape[0] // 2
    onward = [(i, (i + 1) % devices) for i in range(devices)]
    back = [((i + 1) % devices, i) for i in range(devices)]
    return lax.ppermute(rows[:half], BOTH, back), lax.ppermute(rows[half:], BOTH, onward)


def body(
    points,
    cotangent,
    destination,
    curve_slot,
    point_counts,
    shift_offset,
    project_in,
    project_out,
    norm_gain,
):
    devices = lax.axis_size(BOTH)
    groups = lax.axis_size("dp")
    arrived, width = points.shape
    share = project_in.shape[0]
    packed = jnp.concatenate(
        [project_in, project_out, jnp.broadcast_to(norm_gain[:, None], (share, GAIN_COLS))], axis=1
    )
    weights = lax.all_gather(packed, "fsdp", axis=0, tiled=True)
    weights_t = jnp.transpose(weights)
    device = lax.axis_index(BOTH)
    edge_device = jnp.where(2 * shift_offset <= PATCH, devices - 1, 0)
    wrap = (device == edge_device).astype(jnp.int32)

    send_points, target, marks = send_first(
        shift_offset,
        point_counts,
        destination.reshape(1, arrived),
        curve_slot.reshape(1, arrived),
        points,
        devices,
    )
    got_marks = lax.all_to_all(marks, BOTH, split_axis=0, concat_axis=0, tiled=True)
    got_points = exchange(send_points, devices)
    place = place_of(shift_offset, got_marks)
    send_cot = pick(target, cotangent, arrived, "send_cot")
    got_cot = exchange(send_cot, devices)

    own_points = pick(place, got_points, PATCH, "curve_points")
    points_top, points_bottom = neighbours(own_points, devices)
    own_cot = pick(place, got_cot, PATCH, "curve_cot")
    cot_top, cot_bottom = neighbours(own_cot, devices)

    probs, block, *saved = forward(
        shift_offset, wrap, own_points, points_top, points_bottom, weights, weights_t
    )
    block_top, block_bottom = neighbours_back(block, devices)
    back_block = exchange(
        spread_pair(shift_offset, place, block, block_top, block_bottom, "back_block"), devices
    )

    grad, parts = backward(
        shift_offset, own_cot, cot_top, cot_bottom, weights, (probs, *saved)
    )
    grad_top, grad_bottom = neighbours_back(grad, devices)
    back_grad = exchange(
        spread_pair(shift_offset, place, grad, grad_top, grad_bottom, "back_grad"), devices
    )

    shares = lax.psum_scatter(parts, "fsdp", scatter_dimension=0, tiled=True)
    terms = lax.all_to_all(
        shares.reshape(groups, share // groups, shares.shape[1]),
        "dp",
        split_axis=0,
        concat_axis=0,
        tiled=True,
    )
    total = jnp.sum(terms, axis=0)
    totals = lax.all_to_all(
        jnp.broadcast_to(total[None], terms.shape), "dp", split_axis=0, concat_axis=0, tiled=True
    ).reshape(shares.shape)

    block_out = spread(target, back_block, "block_out")
    point_grad = spread(target, back_grad, "point_grad")
    return (
        block_out,
        point_grad,
        totals[:, : 3 * width],
        totals[:, 3 * width : 4 * width],
        totals[:, 4 * width],
    )


def solution(mesh):
    in_specs = (
        P(BOTH, None),
        P(BOTH, None),
        P(BOTH),
        P(BOTH),
        P(BOTH),
        P(),
        P("fsdp", None),
        P("fsdp", None),
        P("fsdp"),
    )
    out_specs = (
        P(BOTH, None),
        P(BOTH, None),
        P("fsdp", None),
        P("fsdp", None),
        P("fsdp"),
    )
    return jax.shard_map(body, mesh=mesh, in_specs=in_specs, out_specs=out_specs, check_vma=False)
```

```python
import functools

import jax
import jax.numpy as jnp
from jax import lax
from jax.experimental import pallas as pl
from jax.experimental.pallas import tpu as pltpu
from jax.sharding import PartitionSpec as P

HEADS = 16
PATCH = 1024
EPS = 1e-05
BOTH = ("dp", "fsdp")
GAIN_COLS = 128
MARK_COLS = 128
LANES = 128
TILE_ROWS = 16
FAR = -1e30
LOG2E = 1.4426950408889634
F32 = jnp.float32
BF16 = jnp.bfloat16
FORWARD_HEADS, FORWARD_CHUNK = 2, 1024
BACKWARD_HEADS, BACKWARD_CHUNK = 1, 512
PROBS = F32
VMEM_BYTES = 63 * 1024 * 1024


def params(steps=1):
    return pltpu.CompilerParams(
        vmem_limit_bytes=VMEM_BYTES, dimension_semantics=("arbitrary",) * steps
    )


def whole(shape):
    zeros = (0,) * len(shape)
    return pl.BlockSpec(shape, lambda *_: zeros)


SMEM = pl.BlockSpec(memory_space=pltpu.SMEM)
ANY = pl.BlockSpec(memory_space=pl.ANY)


def lasting(us):
    return pl.CostEstimate(flops=int(us * 1e9), bytes_accessed=0, transcendentals=0)


def ones_where(mask, dtype=BF16):
    return jnp.where(mask, 1.0, 0.0).astype(dtype)


def iota(shape, dim):
    return lax.broadcasted_iota(jnp.int32, shape, dim)


def nt(a, b):
    return lax.dot_general(a, b, (((1,), (1,)), ((), ())), preferred_element_type=F32)


def nn(a, b):
    return jnp.dot(a, b, preferred_element_type=F32)


def pick_rows(index_row, rows, first, count):
    slots = index_row.shape[1]
    chosen = ones_where(iota((count, slots), 0) + first == index_row)
    return nn(chosen, rows).astype(BF16)


def slot_targets(count, dest_ref, target_ref, devices):
    arrived = dest_ref.shape[1]
    capacity = arrived // devices
    chunk = 256
    before = ones_where(iota((chunk, chunk), 0) < iota((chunk, chunk), 1))
    base = jnp.zeros((devices, 1), F32)
    for start in range(0, arrived, chunk):
        cols = pl.ds(start, chunk)
        dest = dest_ref[:, cols]
        valid = iota((1, chunk), 1) + start < count
        here = jnp.where((iota((devices, chunk), 0) == dest) & valid, 1.0, 0.0)
        ahead = nn(here.astype(BF16), before) + base
        rank = jnp.sum(here * ahead, axis=0, keepdims=True).astype(jnp.int32)
        base = base + jnp.sum(here, axis=1, keepdims=True)
        target_ref[:, cols] = jnp.where(valid, dest * capacity + rank, -1)


def send_first_kernel(devices, shift_ref, count_ref, dest_ref, slot_ref, rows_ref, send_ref, target_ref):
    step = pl.program_id(0)

    @pl.when(step == 0)
    def _():
        slot_targets(count_ref[0], dest_ref, target_ref, devices)

    block = send_ref.shape[0]
    arrived, width = rows_ref.shape
    chosen = ones_where(iota((block, arrived), 0) + step * block == target_ref[...])
    send_ref[:, :width] = nn(chosen, rows_ref[...]).astype(BF16)
    code = jnp.where(slot_ref[...] < shift_ref[0], 2.0, 1.0)
    send_ref[:, width:] = nt(chosen, jnp.broadcast_to(code, (MARK_COLS, arrived)).astype(BF16)).astype(BF16)


def send_first(shift, count, dest, slot, rows, devices, block=512):
    arrived, width = rows.shape
    wide = width + MARK_COLS
    return pl.pallas_call(
        functools.partial(send_first_kernel, devices),
        grid=(arrived // block,),
        in_specs=[SMEM, SMEM, whole((1, arrived)), whole((1, arrived)), whole((arrived, width))],
        out_specs=[pl.BlockSpec((block, wide), lambda i: (i, 0)), whole((1, arrived))],
        out_shape=[
            jax.ShapeDtypeStruct((arrived, wide), BF16),
            jax.ShapeDtypeStruct((1, arrived), jnp.int32),
        ],
        compiler_params=params(),
        cost_estimate=lasting(9),
        name="send_points",
    )(shift, count, dest, slot, rows)


def pick_kernel(index_ref, rows_ref, *refs):
    out_ref = refs[-1]
    block = out_ref.shape[0]
    out_ref[...] = pick_rows(index_ref[...], rows_ref[...], pl.program_id(0) * block, block)


def pick(index, rows, out_rows, name, after=(), block=512):
    arrived, width = rows.shape
    return pl.pallas_call(
        pick_kernel,
        grid=(out_rows // block,),
        in_specs=[whole((1, arrived)), whole((arrived, width))] + [ANY] * len(after),
        out_specs=pl.BlockSpec((block, width), lambda i: (i, 0)),
        out_shape=jax.ShapeDtypeStruct((out_rows, width), BF16),
        compiler_params=params(),
        cost_estimate=lasting(8),
        name=name,
    )(index, rows, *after)


def places(shift, marks_ref, place_ref):
    slots = marks_ref.shape[0]
    marks = jnp.transpose(marks_ref[...].astype(F32))[:1, :]
    chunk = 256
    before = ones_where(iota((chunk, chunk), 0) < iota((chunk, chunk), 1))
    line = iota((8, 1), 0)
    first = lax.convert_element_type(PATCH - shift, F32)
    base = jnp.where(line == 1, first, 0.0)
    for start in range(0, slots, chunk):
        here = marks[:, start : start + chunk]
        flags = jnp.where(here == (line + 1).astype(F32), 1.0, 0.0)
        flags = jnp.where(line < 2, flags, 0.0)
        earlier = nn(flags.astype(BF16), before) + base
        base = base + jnp.sum(flags, axis=1, keepdims=True)
        place = jnp.sum(flags * earlier, axis=0, keepdims=True).astype(jnp.int32)
        place_ref[:, start : start + chunk] = jnp.where(here > 0.0, place, -1)


def land_first_kernel(shift_ref, marks_ref, rows_ref, *refs):
    own_ref, place_ref = refs[-2:]
    places(shift_ref[0], marks_ref, place_ref)
    own_ref[...] = pick_rows(place_ref[...], rows_ref[...], 0, PATCH)


def land_first(shift, got, width, after):
    slots, wide = got.shape
    return pl.pallas_call(
        land_first_kernel,
        grid=(1,),
        in_specs=[
            SMEM,
            pl.BlockSpec((slots, MARK_COLS), lambda i: (0, width // MARK_COLS)),
            pl.BlockSpec((slots, width), lambda i: (0, 0)),
        ]
        + [ANY] * len(after),
        out_specs=[whole((PATCH, width)), whole((1, slots))],
        out_shape=[
            jax.ShapeDtypeStruct((PATCH, width), BF16),
            jax.ShapeDtypeStruct((1, slots), jnp.int32),
        ],
        compiler_params=params(),
        cost_estimate=lasting(7),
        name="land_points",
    )(shift, got, got, *after)


def pack_kernel(in_ref, out_ref, gain_ref, *refs):
    packed_ref = refs[-1]
    inner, outer = in_ref.shape[1], out_ref.shape[1]
    packed_ref[:, :inner] = in_ref[...]
    packed_ref[:, inner : inner + outer] = out_ref[...]
    column = jnp.transpose(jnp.broadcast_to(gain_ref[...].astype(F32), (GAIN_COLS, gain_ref.shape[1])))
    packed_ref[:, inner + outer :] = column.astype(BF16)


def pack(project_in, project_out, gain, after):
    share = project_in.shape[0]
    columns = project_in.shape[1] + project_out.shape[1] + GAIN_COLS
    return pl.pallas_call(
        pack_kernel,
        grid=(1,),
        in_specs=[whole(project_in.shape), whole(project_out.shape), whole((1, share))]
        + [ANY] * len(after),
        out_specs=whole((share, columns)),
        out_shape=jax.ShapeDtypeStruct((share, columns), BF16),
        compiler_params=params(),
        cost_estimate=lasting(1),
        name="pack_weights",
    )(project_in, project_out, gain.reshape(1, share), *after)


def column_of(row):
    length = row.shape[1]
    return jnp.transpose(jnp.broadcast_to(row, (128, length)))


def spread_rows(index_row, rows):
    wide = column_of(index_row)
    count = wide.shape[0]
    lanes = iota((count, 128), 1)
    chosen = jnp.concatenate(
        [ones_where(wide == lanes + start) for start in range(0, rows.shape[0], 128)], axis=1
    )
    return nn(chosen, rows).astype(BF16)


def spread_kernel(index_ref, rows_ref, *refs):
    out_ref = refs[-1]
    out_ref[...] = spread_rows(index_ref[...], rows_ref[...])


def spread(index, rows, width, name, after=(), block=512):
    slots, source = index.shape[1], rows.shape[0]
    return pl.pallas_call(
        spread_kernel,
        grid=(slots // block,),
        in_specs=[pl.BlockSpec((1, block), lambda i: (0, i)), whole((source, width))]
        + [ANY] * len(after),
        out_specs=pl.BlockSpec((block, width), lambda i: (i, 0)),
        out_shape=jax.ShapeDtypeStruct((slots, width), BF16),
        compiler_params=params(),
        cost_estimate=lasting(8),
        name=name,
    )(index, rows, *after)


def spread_pair_kernel(groups, shift_ref, index_ref, own_ref, other_ref, *refs):
    out_ref, rows = refs[-2:]
    step = pl.program_id(0)

    @pl.when(step == 0)
    def _():
        rows[...] = joined(shift_ref[0], own_ref, other_ref)

    width = rows.shape[1]
    out_ref[:, :width] = spread_rows(index_ref[...], rows[...])
    if groups is None:
        return
    shares, of_rows = groups
    across = shares * TILE_ROWS // of_rows
    members = refs[0].shape[0] // of_rows
    blocks = [
        (keep, got, pl.ds(start, LANES))
        for keep, got in (refs[0:2], refs[2:4])
        for start in range(0, keep.shape[1], LANES)
    ]
    for number, (keep, got, lanes) in enumerate(blocks):
        start = width + number // across * LANES
        for f in range(members):
            source = pl.ds(pl.multiple_of(f * of_rows + step * TILE_ROWS, TILE_ROWS), TILE_ROWS)
            to = (number % across * members + f) * TILE_ROWS
            out_ref[to : to + TILE_ROWS, start : start + LANES] = (
                keep[source, lanes] + got[source, lanes]
            ).astype(BF16)


def spread_pair(shift, index, pair, name, parts=(), groups=None, after=()):
    slots = index.shape[1]
    source, width = pair[0].shape
    blocks = groups[1] // TILE_ROWS if parts else 4
    wide = width + sum(part.shape[1] for part in parts[::2]) * LANES // width
    block = slots // blocks
    return pl.pallas_call(
        functools.partial(spread_pair_kernel, groups),
        grid=(blocks,),
        in_specs=[SMEM, pl.BlockSpec((1, block), lambda i: (0, i))]
        + [whole((source, width))] * 2
        + [whole(part.shape) for part in parts]
        + [ANY] * len(after),
        out_specs=pl.BlockSpec((block, wide), lambda i: (i, 0)),
        out_shape=jax.ShapeDtypeStruct((slots, wide), BF16),
        scratch_shapes=[pltpu.VMEM((source, width), BF16)],
        compiler_params=params(),
        cost_estimate=lasting(6),
        name=name,
    )(shift, index, *pair, *parts, *after)


def add_tiles_kernel(tiles_ref, gain_ref, *refs):
    out_ref = refs[-1]
    slots, lanes = tiles_ref.shape
    pairs = tiles_ref[...].astype(F32).reshape(slots // TILE_ROWS // 2, 2, TILE_ROWS, lanes)
    sums = jnp.sum(pairs, axis=0)
    gain = jnp.concatenate([gain_ref[...], jnp.zeros((TILE_ROWS - 8, LANES), F32)], axis=0)
    line = jnp.concatenate([sums[0], sums[1], gain], axis=1)
    out_ref[...] = jnp.broadcast_to(line[None], out_ref.shape)


def add_tiles(got, gain, width, shares, after):
    slots, wide = got.shape
    more = wide - width
    shape = (shares, TILE_ROWS, 2 * more + LANES)
    return pl.pallas_call(
        add_tiles_kernel,
        grid=(1,),
        in_specs=[pl.BlockSpec((slots, more), lambda i: (0, width // more)), whole(gain.shape)]
        + [ANY] * len(after),
        out_specs=whole(shape),
        out_shape=jax.ShapeDtypeStruct(shape, F32),
        compiler_params=params(),
        cost_estimate=lasting(2),
        name="add_tiles",
    )(got, gain, *after)


def settle_kernel(groups, columns, member_ref, tiles_ref, in_ref, out_ref, gain_ref):
    shares, of_rows = groups
    across = shares * TILE_ROWS // of_rows
    width = out_ref.shape[1]
    half = width // 2
    each = (tiles_ref.shape[2] - LANES) // LANES // 2
    for share in range(shares):
        rows = pl.ds(share // across * TILE_ROWS, TILE_ROWS)
        for core in range(2):
            for k in range(each):
                lane = (core * each + k) * LANES
                tile = tiles_ref[share, :, lane : lane + LANES]
                column = (k * across + share % across) * LANES
                group = column // columns[0]
                column = column - group * columns[0] + core * columns[group]
                part, start = column // half, column % half
                if part < 3:
                    start += part * width + group * half
                    in_ref[rows, start : start + LANES] = tile
                else:
                    start = column - 3 * half
                    out_ref[rows, start : start + LANES] = tile
    gains = jnp.sum(tiles_ref[:, :8, 2 * each * LANES :], axis=0)
    a_line = LANES // of_rows
    mine = iota(gains.shape, 0) == lax.div(member_ref[0], a_line)
    line = jnp.sum(jnp.where(mine, gains, 0.0), axis=0, keepdims=True)
    gain_ref[...] = line[:, :of_rows]
    for piece in range(1, a_line):
        @pl.when(lax.rem(member_ref[0], a_line) == piece)
        def _():
            gain_ref[...] = line[:, piece * of_rows : (piece + 1) * of_rows]


def settle(member, tiles, groups, columns, width):
    of_rows = groups[1]
    shapes = [(of_rows, 3 * width), (of_rows, width), (1, of_rows)]
    return pl.pallas_call(
        functools.partial(settle_kernel, groups, columns),
        grid=(1,),
        in_specs=[SMEM, whole(tiles.shape)],
        out_specs=[whole(shape) for shape in shapes],
        out_shape=[jax.ShapeDtypeStruct(shape, F32) for shape in shapes],
        compiler_params=params(),
        cost_estimate=lasting(2),
        name="settle",
    )(member, tiles)


def gate_kernel(*refs):
    pass


def gate(array, *after):
    return pl.pallas_call(
        gate_kernel,
        in_specs=[ANY] * (1 + len(after)),
        out_specs=ANY,
        out_shape=jax.ShapeDtypeStruct(array.shape, array.dtype),
        input_output_aliases={0: 0},
        compiler_params=pltpu.CompilerParams(has_side_effects=True),
        name="gate",
    )(array, *after)


def joined(shift, own_ref, other_ref):
    row = iota(own_ref.shape, 0)
    return jnp.where(row < PATCH - shift, own_ref[...], other_ref[...])


def attend(key_x, query_x, value, probs_ref, out_ref, step):
    heads, head_width, length = value.shape
    scale = head_width ** (-0.5) * LOG2E
    for start in range(0, length, FORWARD_CHUNK):
        cols = pl.ds(start, FORWARD_CHUNK)
        scores = [nn(jnp.transpose(key_x[h]), query_x[h, :, cols]) for h in range(heads)]
        for h in range(heads):
            top = jnp.max(scores[h], axis=0, keepdims=True)
            weights = jnp.exp2((scores[h] - top) * scale)
            probs = weights * (1.0 / jnp.sum(weights, axis=0, keepdims=True))
            rounded = probs.astype(BF16)
            probs_ref[h, :, cols] = probs.astype(PROBS)
            out_ref[step * heads + h, :, cols] = nn(value[h], rounded).astype(BF16)


def forward_first_kernel(
    shift_ref,
    wrap_ref,
    own_ref,
    other_ref,
    in_ref,
    gain_ref,
    probs_ref,
    hidden_ref,
    normed_ref,
    inverse_ref,
    query_x,
    key_x,
    values_ref,
    attended_ref,
):
    step = pl.program_id(0)
    heads, head_width, length = values_ref.shape
    width = heads * head_width
    extra = query_x.shape[1] - head_width

    @pl.when(step == 0)
    def _():
        rows = joined(shift_ref[0], own_ref, other_ref)
        values_in = jnp.transpose(rows.astype(F32))
        center = values_in - jnp.mean(values_in, axis=0, keepdims=True)
        inverse = lax.rsqrt(jnp.mean(center * center, axis=0, keepdims=True) + EPS)
        normed = center * inverse
        normed_ref[...] = normed
        inverse_ref[...] = inverse
        hidden = (normed * gain_ref[:, :1].astype(F32)).astype(BF16)
        hidden_ref[...] = hidden
        for part, ref in enumerate((query_x, key_x, values_ref)):
            columns = in_ref[:, part * width : (part + 1) * width]
            made = nn(jnp.transpose(columns), hidden).astype(BF16)
            ref[:, :head_width, :] = made.reshape(heads, head_width, length)
        side = iota((extra, length), 1) >= PATCH - shift_ref[0]
        line = iota((extra, length), 0)
        query_side = jnp.where(((line == 0) & ~side) | ((line == 1) & side), 1.0, 0.0)
        key_side = jnp.where(((line == 0) & side) | ((line == 1) & ~side), FAR, 0.0)
        key_side = jnp.where(wrap_ref[0] > 0, key_side, 0.0)
        for h in range(heads):
            query_x[h, head_width:, :] = query_side.astype(BF16)
            key_x[h, head_width:, :] = key_side.astype(BF16)

    count = probs_ref.shape[0]
    mine = pl.ds(step * count, count)
    attend(key_x.at[mine], query_x.at[mine], values_ref.at[mine], probs_ref, attended_ref, step)


def forward_last_kernel(
    shift_ref,
    own_ref,
    other_ref,
    out_ref,
    query_x,
    key_x,
    value_ref,
    first_ref,
    probs_ref,
    attended_ref,
    block_ref,
):
    step = pl.program_id(0)
    length, width = own_ref.shape
    attend(key_x, query_x, value_ref, probs_ref, attended_ref, step)

    @pl.when(step == pl.num_programs(0) - 1)
    def _():
        rows = joined(shift_ref[0], own_ref, other_ref)
        attended = jnp.concatenate(
            [r[...].reshape(width // 2, length) for r in (first_ref, attended_ref)], axis=0
        )
        added = nn(jnp.transpose(out_ref[...]), attended)
        block_ref[...] = (rows.astype(F32) + jnp.transpose(added)).astype(BF16)


def per_step(shape, first):
    return pl.BlockSpec(shape, lambda i: (i + first, 0, 0))


def forward(shift, wrap, pair, weights):
    length, width = pair[0].shape
    head_width = width // HEADS
    some = HEADS // 2
    count = FORWARD_HEADS
    extended = (HEADS, head_width + 16, length)
    split = (HEADS, head_width, length)
    first_split = (some, head_width, length)
    rows_specs = [whole((length, width))] * 2
    probs_a, hidden, normed, inverse, query_x, key_x, values, attended_a = pl.pallas_call(
        forward_first_kernel,
        grid=(some // count,),
        in_specs=[SMEM, SMEM]
        + rows_specs
        + [
            pl.BlockSpec((width, 3 * width), lambda h: (0, 0)),
            pl.BlockSpec((width, GAIN_COLS), lambda h: (0, 4 * width // GAIN_COLS)),
        ],
        out_specs=[
            per_step((count, length, length), 0),
            whole((width, length)),
            whole((width, length)),
            whole((1, length)),
            whole(extended),
            whole(extended),
            whole(split),
            whole(first_split),
        ],
        out_shape=[
            jax.ShapeDtypeStruct((some, length, length), PROBS),
            jax.ShapeDtypeStruct((width, length), BF16),
            jax.ShapeDtypeStruct((width, length), F32),
            jax.ShapeDtypeStruct((1, length), F32),
            jax.ShapeDtypeStruct(extended, BF16),
            jax.ShapeDtypeStruct(extended, BF16),
            jax.ShapeDtypeStruct(split, BF16),
            jax.ShapeDtypeStruct(first_split, BF16),
        ],
        compiler_params=params(),
        cost_estimate=lasting(25),
        name="forward_first",
    )(shift, wrap, *pair, weights, weights)
    skip = some // count
    probs_b, attended_b, block = pl.pallas_call(
        forward_last_kernel,
        grid=(some // count,),
        in_specs=[SMEM]
        + rows_specs
        + [
            pl.BlockSpec((width, width), lambda h: (0, 3)),
            per_step((count,) + extended[1:], skip),
            per_step((count,) + extended[1:], skip),
            per_step((count,) + split[1:], skip),
            whole(first_split),
        ],
        out_specs=[
            per_step((count, length, length), 0),
            whole(first_split),
            whole((length, width)),
        ],
        out_shape=[
            jax.ShapeDtypeStruct((some, length, length), PROBS),
            jax.ShapeDtypeStruct(first_split, BF16),
            jax.ShapeDtypeStruct((length, width), BF16),
        ],
        compiler_params=params(),
        cost_estimate=lasting(20),
        name="forward_last",
    )(shift, *pair, weights, query_x, key_x, values, attended_a)
    return block, (probs_a, probs_b), (query_x, key_x, values), (attended_a, attended_b), (
        hidden,
        normed,
        inverse,
    )


def attend_back(probs_ref, query_x, key_x, values_ref, attended_ref, upstream_ref, grads_ref, step):
    heads, head_width, length = values_ref.shape
    scale = head_width ** (-0.5)
    for h in range(heads):
        query, key, value = query_x[h, :head_width, :], key_x[h, :head_width, :], values_ref[h]
        upstream = upstream_ref[h]
        value_rows = jnp.transpose(value)
        offset = jnp.sum(
            upstream.astype(F32) * attended_ref[h].astype(F32), axis=0, keepdims=True
        )
        head = step * heads + h
        key_grad = value_grad = 0.0
        for start in range(0, length, BACKWARD_CHUNK):
            cols = slice(start, start + BACKWARD_CHUNK)
            probs = probs_ref[h, :, cols]
            along = nn(value_rows, upstream[:, cols])
            slopes = (probs.astype(F32) * (along - offset[:, cols]) * scale).astype(BF16)
            grads_ref[0, head, :, cols] = nn(key, slopes).astype(BF16)
            key_grad = key_grad + nt(query[:, cols], slopes)
            value_grad = value_grad + nt(upstream[:, cols], probs.astype(BF16))
        grads_ref[1, head] = key_grad.astype(BF16)
        grads_ref[2, head] = value_grad.astype(BF16)


def backward_first_kernel(
    shift_ref,
    own_ref,
    other_ref,
    out_ref,
    probs_ref,
    query_x,
    key_x,
    values_ref,
    attended_ref,
    hidden_ref,
    attended_a_ref,
    attended_b_ref,
    core_ref,
    cot_ref,
    upstream_b_ref,
    grads_ref,
    keep_ref,
    send_ref,
    upstream_a,
):
    step = pl.program_id(0)
    some, head_width, length = upstream_a.shape
    count = probs_ref.shape[0]

    @pl.when(step == 0)
    def _():
        rows = joined(shift_ref[0], own_ref, other_ref)
        cot_ref[...] = rows
        upstream = nt(out_ref[...], rows).astype(BF16).reshape(2, some, head_width, length)
        upstream_a[...] = upstream[0]
        upstream_b_ref[...] = upstream[1]

    attend_back(
        probs_ref,
        query_x,
        key_x,
        values_ref,
        attended_ref,
        upstream_a.at[pl.ds(step * count, count)],
        grads_ref,
        step,
    )

    @pl.when(step == pl.num_programs(0) - 1)
    def _():
        width = cot_ref.shape[1]
        part_in = nt(hidden_ref[...], grads_ref[...].reshape(3 * width // 2, length))
        part_out = [
            nn(out[...].reshape(width // 2, length), cot_ref[...])
            for out in (attended_a_ref, attended_b_ref)
        ]
        parts = jnp.concatenate([part_in, jnp.concatenate(part_out, axis=0)], axis=1)
        keep_and_send(core_ref[0], parts, keep_ref, send_ref)


def keep_and_send(core, parts, keep_ref, send_ref):
    half = parts.shape[1] // 2
    first, second = parts[:, :half], parts[:, half:]
    keep_ref[...] = jnp.where(core == 0, first, second)
    send_ref[...] = jnp.where(core == 0, second, first)


def backward_last_kernel(
    in_ref,
    gain_ref,
    probs_ref,
    hidden_ref,
    normed_ref,
    inverse_ref,
    query_x,
    key_x,
    values_ref,
    attended_ref,
    upstream_ref,
    first_ref,
    cot_ref,
    core_ref,
    *refs,
):
    grad_ref, keep_ref, send_ref, gain_out, grads = refs[-5:]
    step = pl.program_id(0)
    length, width = cot_ref.shape
    half = width // 2
    attend_back(
        probs_ref, query_x, key_x, values_ref, attended_ref, upstream_ref, grads, step
    )

    @pl.when(step == pl.num_programs(0) - 1)
    def _():
        grad_hidden = 0.0
        for group, ref in enumerate((first_ref, grads)):
            for part in range(3):
                first = part * width + group * half
                grad_hidden = grad_hidden + nn(
                    in_ref[:, first : first + half], ref[part].reshape(half, length)
                )
        parts = nt(hidden_ref[...], grads[...].reshape(3 * half, length))
        keep_and_send(core_ref[0], parts, keep_ref, send_ref)
        normed = normed_ref[...]
        part_gain = jnp.sum(grad_hidden * normed, axis=1, keepdims=True)
        part_gain = jnp.transpose(jnp.broadcast_to(part_gain, (width, LANES)))[:1, :]
        lines = [part_gain[:, start : start + LANES] for start in range(0, width, LANES)]
        lines.append(jnp.zeros((8 - len(lines), LANES), F32))
        gain_out[...] = jnp.concatenate(lines, axis=0)
        scaled = grad_hidden * gain_ref[:, :1].astype(F32)
        middle = jnp.mean(scaled, axis=0, keepdims=True)
        slope = jnp.mean(scaled * normed, axis=0, keepdims=True)
        change = inverse_ref[...] * (scaled - middle - normed * slope)
        grad_ref[...] = (cot_ref[...].astype(F32) + jnp.transpose(change)).astype(BF16)


def backward_first(shift, pair, weights, probs, split, attended, hidden, core):
    length, width = pair[0].shape
    head_width = width // HEADS
    some = HEADS // 2
    count = BACKWARD_HEADS
    group = (some, head_width, length)
    extended = (count, head_width + 16, length)
    return pl.pallas_call(
        backward_first_kernel,
        grid=(some // count,),
        in_specs=[
            SMEM,
            whole((length, width)),
            whole((length, width)),
            pl.BlockSpec((width, width), lambda h: (0, 3)),
            per_step((count, length, length), 0),
            per_step(extended, 0),
            per_step(extended, 0),
            per_step((count, head_width, length), 0),
            per_step((count, head_width, length), 0),
            whole((width, length)),
            whole(group),
            whole(group),
            SMEM,
        ],
        out_specs=[
            whole((length, width)),
            whole(group),
            whole((3,) + group),
            whole((width, 5 * width // 4)),
            whole((width, 5 * width // 4)),
        ],
        out_shape=[
            jax.ShapeDtypeStruct((length, width), BF16),
            jax.ShapeDtypeStruct(group, BF16),
            jax.ShapeDtypeStruct((3,) + group, BF16),
            jax.ShapeDtypeStruct((width, 5 * width // 4), F32),
            jax.ShapeDtypeStruct((width, 5 * width // 4), F32),
        ],
        scratch_shapes=[pltpu.VMEM(group, BF16)],
        compiler_params=params(),
        cost_estimate=lasting(25),
        name="backward_first",
    )(shift, *pair, weights, probs, *split, attended[0], hidden, *attended, core)


def backward_last(weights, probs, rows, split, attended, upstream, first, cot, core, after):
    length, width = cot.shape
    head_width = width // HEADS
    some = HEADS // 2
    count = BACKWARD_HEADS
    skip = some // count
    group = (some, head_width, length)
    extended = (count, head_width + 16, length)
    one = (count, head_width, length)
    return pl.pallas_call(
        backward_last_kernel,
        grid=(some // count,),
        in_specs=[
            pl.BlockSpec((width, 3 * width), lambda h: (0, 0)),
            pl.BlockSpec((width, GAIN_COLS), lambda h: (0, 4 * width // GAIN_COLS)),
            per_step((count, length, length), 0),
            whole((width, length)),
            whole((width, length)),
            whole((1, length)),
            per_step(extended, skip),
            per_step(extended, skip),
            per_step(one, skip),
            per_step(one, 0),
            per_step(one, 0),
            whole((3,) + group),
            whole((length, width)),
            SMEM,
        ]
        + [ANY] * len(after),
        out_specs=[
            whole((length, width)),
            whole((width, 3 * width // 4)),
            whole((width, 3 * width // 4)),
            whole((8, LANES)),
        ],
        out_shape=[
            jax.ShapeDtypeStruct((length, width), BF16),
            jax.ShapeDtypeStruct((width, 3 * width // 4), F32),
            jax.ShapeDtypeStruct((width, 3 * width // 4), F32),
            jax.ShapeDtypeStruct((8, LANES), F32),
        ],
        scratch_shapes=[pltpu.VMEM((3,) + group, BF16)],
        compiler_params=params(),
        cost_estimate=lasting(25),
        name="backward_last",
    )(
        weights,
        weights,
        probs,
        *rows,
        *split,
        attended[1],
        upstream,
        first,
        cot,
        core,
        *after,
    )


def exchange(rows, devices):
    moved = lax.all_to_all(
        rows.reshape(devices, rows.shape[0] // devices, rows.shape[1]),
        BOTH,
        split_axis=0,
        concat_axis=0,
        tiled=True,
    )
    return moved.reshape(rows.shape)


def with_ahead(rows, devices):
    pairs = [((i + 1) % devices, i) for i in range(devices)]
    return rows, lax.ppermute(rows, BOTH, pairs)


def with_behind(rows, devices):
    pairs = [(i, (i + 1) % devices) for i in range(devices)]
    return rows, lax.ppermute(rows, BOTH, pairs)


def other_core(array):
    pairs = [(i, i ^ 1) for i in range(lax.axis_size("fsdp"))]
    return lax.ppermute(array, "fsdp", pairs)


def over_fsdp(terms):
    count, far = lax.axis_size("fsdp"), 1
    while far < count:
        terms = terms + lax.ppermute(terms, "fsdp", [(i, i ^ far) for i in range(count)])
        far *= 2
    return terms


def body(
    points,
    cotangent,
    destination,
    curve_slot,
    point_counts,
    shift_offset,
    project_in,
    project_out,
    norm_gain,
):
    devices = lax.axis_size(BOTH)
    groups = lax.axis_size("dp")
    arrived, width = points.shape
    share = project_in.shape[0]
    device = lax.axis_index(BOTH)
    wrap = (device == devices - 1).astype(jnp.int32).reshape(1)

    send_points, target = send_first(
        shift_offset,
        point_counts,
        destination.reshape(1, arrived),
        curve_slot.reshape(1, arrived),
        points,
        devices,
    )
    got_points = exchange(send_points, devices)
    packed = pack(project_in, project_out, norm_gain, (target,))
    weights = lax.all_gather(packed, "fsdp", axis=0, tiled=True)
    send_cot = pick(target, cotangent, arrived, "send_cot")
    own_points, place = land_first(shift_offset, got_points, width, (send_cot,))
    points_pair = with_ahead(own_points, devices)
    got_cot = exchange(gate(send_cot, points_pair[1]), devices)

    block, (probs_a, probs_b), split, attended, (hidden, normed, inverse) = forward(
        shift_offset, wrap, points_pair, weights
    )
    own_cot = pick(place, got_cot, PATCH, "land_cot", (probs_a,), PATCH)
    cot_pair = with_ahead(own_cot, devices)
    block_pair = with_behind(block, devices)

    member = lax.axis_index("fsdp").astype(jnp.int32)
    core = (member % 2).reshape(1)
    cot, upstream, first_grads, first_keep, first_send = backward_first(
        shift_offset, cot_pair, weights, probs_a, split, attended, hidden, core
    )
    spread_block = spread_pair(shift_offset, place, block_pair, "back_block", after=(first_grads,))
    back_block = exchange(spread_block, devices)
    grad, last_keep, last_send, part_gain = backward_last(
        weights,
        probs_b,
        (hidden, normed, inverse),
        split,
        attended,
        upstream,
        first_grads,
        cot,
        core,
        (spread_block,),
    )
    grad_pair = with_behind(grad, devices)
    dealt = (groups, share)
    parts = (first_keep, other_core(first_send), last_keep, other_core(last_send))
    gain_terms = over_fsdp(part_gain)
    spread_grad = spread_pair(
        shift_offset, place, grad_pair, "back_grad", parts, dealt, (back_block, gain_terms)
    )
    back_grad = exchange(spread_grad, devices)
    block_out = spread(target, back_block, width, "block_out", (spread_grad,))
    sums = add_tiles(back_grad, gain_terms, width, groups, (block_out,))
    tiles = lax.all_to_all(sums, "dp", split_axis=0, concat_axis=0, tiled=True)
    point_grad = spread(target, back_grad, width, "point_grad", (sums,))
    columns = (first_keep.shape[1], last_keep.shape[1])
    grad_in, grad_out, grad_gain = settle(member.reshape(1), tiles, dealt, columns, width)
    return block_out, point_grad, grad_in, grad_out, grad_gain.reshape(share)


def solution(mesh):
    in_specs = (
        P(BOTH, None),
        P(BOTH, None),
        P(BOTH),
        P(BOTH),
        P(BOTH),
        P(),
        P("fsdp", None),
        P("fsdp", None),
        P("fsdp"),
    )
    out_specs = (
        P(BOTH, None),
        P(BOTH, None),
        P("fsdp", None),
        P("fsdp", None),
        P("fsdp"),
    )
    return jax.shard_map(body, mesh=mesh, in_specs=in_specs, out_specs=out_specs, check_vma=False)
```

```python
import functools

import jax
import jax.numpy as jnp
from jax import lax
from jax.experimental import pallas as pl
from jax.experimental.pallas import tpu as pltpu
from jax.sharding import PartitionSpec as P

HEADS = 16
PATCH = 1024
EPS = 1e-05
BOTH = ("dp", "fsdp")
GAIN_COLS = 128
MARK_COLS = 128
LANES = 128
TILE_ROWS = 16
FAR = -1e30
LOG2E = 1.4426950408889634
F32 = jnp.float32
BF16 = jnp.bfloat16
FORWARD_HEADS, FORWARD_CHUNK = 2, 1024
BACKWARD_HEADS, BACKWARD_CHUNK = 1, 512
PROBS = F32
VMEM_BYTES = 63 * 1024 * 1024


def params(steps=1):
    return pltpu.CompilerParams(
        vmem_limit_bytes=VMEM_BYTES, dimension_semantics=("arbitrary",) * steps
    )


def whole(shape):
    zeros = (0,) * len(shape)
    return pl.BlockSpec(shape, lambda *_: zeros)


SMEM = pl.BlockSpec(memory_space=pltpu.SMEM)
ANY = pl.BlockSpec(memory_space=pl.ANY)


def lasting(us):
    return pl.CostEstimate(flops=int(us * 1e9), bytes_accessed=0, transcendentals=0)


def ones_where(mask, dtype=BF16):
    return jnp.where(mask, 1.0, 0.0).astype(dtype)


def iota(shape, dim):
    return lax.broadcasted_iota(jnp.int32, shape, dim)


def nt(a, b):
    return lax.dot_general(a, b, (((1,), (1,)), ((), ())), preferred_element_type=F32)


def nn(a, b):
    return jnp.dot(a, b, preferred_element_type=F32)


def pick_rows(index_row, rows, first, count):
    slots = index_row.shape[1]
    chosen = ones_where(iota((count, slots), 0) + first == index_row)
    return nn(chosen, rows).astype(BF16)


def seat(shard):
    core, along_y = shard & 1, (shard >> 1) & 3
    along_z, along_x = (shard >> 3) & 3, shard >> 5
    y, z = (along_y - along_z) & 3, (along_z - along_x) & 3
    return (((along_x << 2) + z << 2) + y << 1) + core


def slot_targets(count, dest_ref, target_ref, devices):
    arrived = dest_ref.shape[1]
    capacity = arrived // devices
    chunk = 256
    before = ones_where(iota((chunk, chunk), 0) < iota((chunk, chunk), 1))
    base = jnp.zeros((devices, 1), F32)
    for start in range(0, arrived, chunk):
        cols = pl.ds(start, chunk)
        dest = seat(dest_ref[:, cols])
        valid = iota((1, chunk), 1) + start < count
        here = jnp.where((iota((devices, chunk), 0) == dest) & valid, 1.0, 0.0)
        ahead = nn(here.astype(BF16), before) + base
        rank = jnp.sum(here * ahead, axis=0, keepdims=True).astype(jnp.int32)
        base = base + jnp.sum(here, axis=1, keepdims=True)
        target_ref[:, cols] = jnp.where(valid, dest * capacity + rank, -1)


def send_first_kernel(devices, shift_ref, count_ref, dest_ref, slot_ref, rows_ref, *refs):
    send_ref, target_ref = refs[-2:]
    step = pl.program_id(0)

    @pl.when(step == 0)
    def _():
        slot_targets(count_ref[0], dest_ref, target_ref, devices)

    block = send_ref.shape[0]
    arrived, width = rows_ref.shape
    chosen = ones_where(iota((block, arrived), 0) + step * block == target_ref[...])
    send_ref[:, :width] = nn(chosen, rows_ref[...]).astype(BF16)
    code = jnp.where(slot_ref[...] < shift_ref[0], 2.0, 1.0)
    send_ref[:, width:] = nt(chosen, jnp.broadcast_to(code, (MARK_COLS, arrived)).astype(BF16)).astype(BF16)


def send_first(shift, count, dest, slot, rows, devices, after, block=512):
    arrived, width = rows.shape
    wide = width + MARK_COLS
    return pl.pallas_call(
        functools.partial(send_first_kernel, devices),
        grid=(arrived // block,),
        in_specs=[SMEM, SMEM, whole((1, arrived)), whole((1, arrived)), whole((arrived, width))]
        + [ANY] * len(after),
        out_specs=[pl.BlockSpec((block, wide), lambda i: (i, 0)), whole((1, arrived))],
        out_shape=[
            jax.ShapeDtypeStruct((arrived, wide), BF16),
            jax.ShapeDtypeStruct((1, arrived), jnp.int32),
        ],
        compiler_params=params(),
        cost_estimate=lasting(9),
        name="send_points",
    )(shift, count, dest, slot, rows, *after)


def pick_kernel(index_ref, rows_ref, *refs):
    out_ref = refs[-1]
    block = out_ref.shape[0]
    out_ref[...] = pick_rows(index_ref[...], rows_ref[...], pl.program_id(0) * block, block)


def pick(index, rows, out_rows, name, after=(), block=512):
    arrived, width = rows.shape
    return pl.pallas_call(
        pick_kernel,
        grid=(out_rows // block,),
        in_specs=[whole((1, arrived)), whole((arrived, width))] + [ANY] * len(after),
        out_specs=pl.BlockSpec((block, width), lambda i: (i, 0)),
        out_shape=jax.ShapeDtypeStruct((out_rows, width), BF16),
        compiler_params=params(),
        cost_estimate=lasting(8),
        name=name,
    )(index, rows, *after)


def places(shift, marks_ref, place_ref):
    slots = marks_ref.shape[0]
    marks = jnp.transpose(marks_ref[...].astype(F32))[:1, :]
    chunk = 256
    before = ones_where(iota((chunk, chunk), 0) < iota((chunk, chunk), 1))
    line = iota((8, 1), 0)
    first = lax.convert_element_type(PATCH - shift, F32)
    base = jnp.where(line == 1, first, 0.0)
    for start in range(0, slots, chunk):
        here = marks[:, start : start + chunk]
        flags = jnp.where(here == (line + 1).astype(F32), 1.0, 0.0)
        flags = jnp.where(line < 2, flags, 0.0)
        earlier = nn(flags.astype(BF16), before) + base
        base = base + jnp.sum(flags, axis=1, keepdims=True)
        place = jnp.sum(flags * earlier, axis=0, keepdims=True).astype(jnp.int32)
        place_ref[:, start : start + chunk] = jnp.where(here > 0.0, place, -1)


def halves_out(first, second, index_row, rows):
    half = first.shape[0]
    first[...] = pick_rows(index_row, rows, 0, half)
    second[...] = pick_rows(index_row, rows, half, half)


def land_first_kernel(shift_ref, marks_ref, rows_ref, *refs):
    first_ref, second_ref, place_ref = refs[-3:]
    places(shift_ref[0], marks_ref, place_ref)
    halves_out(first_ref, second_ref, place_ref[...], rows_ref[...])


def land_first(shift, got, width, after):
    slots, wide = got.shape
    half = PATCH // 2
    return pl.pallas_call(
        land_first_kernel,
        grid=(1,),
        in_specs=[
            SMEM,
            pl.BlockSpec((slots, MARK_COLS), lambda i: (0, width // MARK_COLS)),
            pl.BlockSpec((slots, width), lambda i: (0, 0)),
        ]
        + [ANY] * len(after),
        out_specs=[whole((half, width)), whole((half, width)), whole((1, slots))],
        out_shape=[
            jax.ShapeDtypeStruct((half, width), BF16),
            jax.ShapeDtypeStruct((half, width), BF16),
            jax.ShapeDtypeStruct((1, slots), jnp.int32),
        ],
        compiler_params=params(),
        cost_estimate=lasting(7),
        name="land_points",
    )(shift, got, got, *after)


def land_second_kernel(place_ref, rows_ref, *refs):
    first_ref, second_ref = refs[-2:]
    halves_out(first_ref, second_ref, place_ref[...], rows_ref[...])


def land_second(place, got, after):
    slots, width = got.shape
    half = PATCH // 2
    return pl.pallas_call(
        land_second_kernel,
        grid=(1,),
        in_specs=[whole((1, slots)), whole((slots, width))] + [ANY] * len(after),
        out_specs=[whole((half, width)), whole((half, width))],
        out_shape=[jax.ShapeDtypeStruct((half, width), BF16)] * 2,
        compiler_params=params(),
        cost_estimate=lasting(5),
        name="land_cot",
    )(place, got, *after)


def pack_kernel(in_ref, out_ref, gain_ref, packed_ref):
    inner, outer = in_ref.shape[1], out_ref.shape[1]
    packed_ref[:, :inner] = in_ref[...]
    packed_ref[:, inner : inner + outer] = out_ref[...]
    column = jnp.transpose(jnp.broadcast_to(gain_ref[...].astype(F32), (GAIN_COLS, gain_ref.shape[1])))
    packed_ref[:, inner + outer :] = column.astype(BF16)


def pack(project_in, project_out, gain):
    share = project_in.shape[0]
    columns = project_in.shape[1] + project_out.shape[1] + GAIN_COLS
    return pl.pallas_call(
        pack_kernel,
        grid=(1,),
        in_specs=[whole(project_in.shape), whole(project_out.shape), whole((1, share))],
        out_specs=whole((share, columns)),
        out_shape=jax.ShapeDtypeStruct((share, columns), BF16),
        compiler_params=params(),
        cost_estimate=lasting(1),
        name="pack_weights",
    )(project_in, project_out, gain.reshape(1, share))


def column_of(row):
    length = row.shape[1]
    return jnp.transpose(jnp.broadcast_to(row, (128, length)))


def spread_rows(index_row, rows):
    wide = column_of(index_row)
    count = wide.shape[0]
    lanes = iota((count, 128), 1)
    chosen = jnp.concatenate(
        [ones_where(wide == lanes + start) for start in range(0, rows.shape[0], 128)], axis=1
    )
    return nn(chosen, rows).astype(BF16)


def spread_kernel(index_ref, rows_ref, *refs):
    out_ref = refs[-1]
    out_ref[...] = spread_rows(index_ref[...], rows_ref[...])


def spread(index, rows, width, name, after=(), block=512):
    slots, source = index.shape[1], rows.shape[0]
    return pl.pallas_call(
        spread_kernel,
        grid=(slots // block,),
        in_specs=[pl.BlockSpec((1, block), lambda i: (0, i)), whole((source, width))]
        + [ANY] * len(after),
        out_specs=pl.BlockSpec((block, width), lambda i: (i, 0)),
        out_shape=jax.ShapeDtypeStruct((slots, width), BF16),
        compiler_params=params(),
        cost_estimate=lasting(8),
        name=name,
    )(index, rows, *after)


def spread_pair_kernel(groups, shift_ref, index_ref, first_rows, second_rows, top_ref, bottom_ref, *refs):
    out_ref, rows = refs[-2:]
    step = pl.program_id(0)

    @pl.when(step == 0)
    def _():
        rows[...] = joined(shift_ref[0], first_rows, second_rows, top_ref, bottom_ref)

    width = rows.shape[1]
    out_ref[:, :width] = spread_rows(index_ref[...], rows[...])
    if groups is None:
        return
    shares, of_rows = groups
    across = shares * TILE_ROWS // of_rows
    members = refs[0].shape[0] // of_rows
    blocks = [
        (keep, got, pl.ds(start, LANES))
        for keep, got in (refs[0:2], refs[2:4])
        for start in range(0, keep.shape[1], LANES)
    ]
    for number, (keep, got, lanes) in enumerate(blocks):
        start = width + number // across * LANES
        for f in range(members):
            source = pl.ds(pl.multiple_of(f * of_rows + step * TILE_ROWS, TILE_ROWS), TILE_ROWS)
            to = (number % across * members + f) * TILE_ROWS
            out_ref[to : to + TILE_ROWS, start : start + LANES] = (
                keep[source, lanes] + got[source, lanes]
            ).astype(BF16)


def spread_pair(shift, index, pair, name, parts=(), groups=None, after=()):
    slots = index.shape[1]
    half, width = pair[0].shape
    blocks = groups[1] // TILE_ROWS if parts else 4
    wide = width + sum(part.shape[1] for part in parts[::2]) * LANES // width
    block = slots // blocks
    return pl.pallas_call(
        functools.partial(spread_pair_kernel, groups),
        grid=(blocks,),
        in_specs=[SMEM, pl.BlockSpec((1, block), lambda i: (0, i))]
        + [whole((half, width))] * 4
        + [whole(part.shape) for part in parts]
        + [ANY] * len(after),
        out_specs=pl.BlockSpec((block, wide), lambda i: (i, 0)),
        out_shape=jax.ShapeDtypeStruct((slots, wide), BF16),
        scratch_shapes=[pltpu.VMEM((2 * half, width), BF16)],
        compiler_params=params(),
        cost_estimate=lasting(6),
        name=name,
    )(shift, index, *pair, *parts, *after)


def add_tiles_kernel(tiles_ref, gain_ref, *refs):
    out_ref = refs[-1]
    slots, lanes = tiles_ref.shape
    pairs = tiles_ref[...].astype(F32).reshape(slots // TILE_ROWS // 2, 2, TILE_ROWS, lanes)
    sums = jnp.sum(pairs, axis=0)
    gain = jnp.concatenate([gain_ref[...], jnp.zeros((TILE_ROWS - 8, LANES), F32)], axis=0)
    line = jnp.concatenate([sums[0], sums[1], gain], axis=1)
    out_ref[...] = jnp.broadcast_to(line[None], out_ref.shape)


def add_tiles(got, gain, width, shares, after):
    slots, wide = got.shape
    more = wide - width
    shape = (shares, TILE_ROWS, 2 * more + LANES)
    return pl.pallas_call(
        add_tiles_kernel,
        grid=(1,),
        in_specs=[pl.BlockSpec((slots, more), lambda i: (0, width // more)), whole(gain.shape)]
        + [ANY] * len(after),
        out_specs=whole(shape),
        out_shape=jax.ShapeDtypeStruct(shape, F32),
        compiler_params=params(),
        cost_estimate=lasting(2),
        name="add_tiles",
    )(got, gain, *after)


def settle_kernel(groups, columns, member_ref, tiles_ref, in_ref, out_ref, gain_ref):
    shares, of_rows = groups
    across = shares * TILE_ROWS // of_rows
    width = out_ref.shape[1]
    half = width // 2
    each = (tiles_ref.shape[2] - LANES) // LANES // 2
    for share in range(shares):
        rows = pl.ds(share // across * TILE_ROWS, TILE_ROWS)
        for core in range(2):
            for k in range(each):
                lane = (core * each + k) * LANES
                tile = tiles_ref[share, :, lane : lane + LANES]
                column = (k * across + share % across) * LANES
                group = column // columns[0]
                column = column - group * columns[0] + core * columns[group]
                part, start = column // half, column % half
                if part < 3:
                    start += part * width + group * half
                    in_ref[rows, start : start + LANES] = tile
                else:
                    start = column - 3 * half
                    out_ref[rows, start : start + LANES] = tile
    gains = jnp.sum(tiles_ref[:, :8, 2 * each * LANES :], axis=0)
    a_line = LANES // of_rows
    mine = iota(gains.shape, 0) == lax.div(member_ref[0], a_line)
    line = jnp.sum(jnp.where(mine, gains, 0.0), axis=0, keepdims=True)
    gain_ref[...] = line[:, :of_rows]
    for piece in range(1, a_line):
        @pl.when(lax.rem(member_ref[0], a_line) == piece)
        def _():
            gain_ref[...] = line[:, piece * of_rows : (piece + 1) * of_rows]


def settle(member, tiles, groups, columns, width):
    of_rows = groups[1]
    shapes = [(of_rows, 3 * width), (of_rows, width), (1, of_rows)]
    return pl.pallas_call(
        functools.partial(settle_kernel, groups, columns),
        grid=(1,),
        in_specs=[SMEM, whole(tiles.shape)],
        out_specs=[whole(shape) for shape in shapes],
        out_shape=[jax.ShapeDtypeStruct(shape, F32) for shape in shapes],
        compiler_params=params(),
        cost_estimate=lasting(2),
        name="settle",
    )(member, tiles)


def joined(shift, first_ref, second_ref, top_ref, bottom_ref):
    half, width = top_ref.shape
    edge = PATCH - shift
    row = iota((half, width), 0)
    first = jnp.where((2 * shift > PATCH) & (row < edge), top_ref[...], first_ref[...])
    second = jnp.where((2 * shift <= PATCH) & (row + half >= edge), bottom_ref[...], second_ref[...])
    return jnp.concatenate([first, second], axis=0)


def attend(key_x, query_x, value, probs_ref, out_ref, step):
    heads, head_width, length = value.shape
    scale = head_width ** (-0.5) * LOG2E
    for start in range(0, length, FORWARD_CHUNK):
        cols = pl.ds(start, FORWARD_CHUNK)
        scores = [nn(jnp.transpose(key_x[h]), query_x[h, :, cols]) for h in range(heads)]
        for h in range(heads):
            top = jnp.max(scores[h], axis=0, keepdims=True)
            weights = jnp.exp2((scores[h] - top) * scale)
            probs = weights * (1.0 / jnp.sum(weights, axis=0, keepdims=True))
            rounded = probs.astype(BF16)
            probs_ref[h, :, cols] = probs.astype(PROBS)
            out_ref[step * heads + h, :, cols] = nn(value[h], rounded).astype(BF16)


def forward_first_kernel(
    shift_ref,
    wrap_ref,
    first_rows,
    second_rows,
    top_ref,
    bottom_ref,
    in_ref,
    gain_ref,
    probs_ref,
    hidden_ref,
    normed_ref,
    inverse_ref,
    query_x,
    key_x,
    values_ref,
    attended_ref,
):
    step = pl.program_id(0)
    heads, head_width, length = values_ref.shape
    width = heads * head_width
    extra = query_x.shape[1] - head_width

    @pl.when(step == 0)
    def _():
        rows = joined(shift_ref[0], first_rows, second_rows, top_ref, bottom_ref)
        values_in = jnp.transpose(rows.astype(F32))
        center = values_in - jnp.mean(values_in, axis=0, keepdims=True)
        inverse = lax.rsqrt(jnp.mean(center * center, axis=0, keepdims=True) + EPS)
        normed = center * inverse
        normed_ref[...] = normed
        inverse_ref[...] = inverse
        hidden = (normed * gain_ref[:, :1].astype(F32)).astype(BF16)
        hidden_ref[...] = hidden
        for part, ref in enumerate((query_x, key_x, values_ref)):
            columns = in_ref[:, part * width : (part + 1) * width]
            made = nn(jnp.transpose(columns), hidden).astype(BF16)
            ref[:, :head_width, :] = made.reshape(heads, head_width, length)
        side = iota((extra, length), 1) >= PATCH - shift_ref[0]
        line = iota((extra, length), 0)
        query_side = jnp.where(((line == 0) & ~side) | ((line == 1) & side), 1.0, 0.0)
        key_side = jnp.where(((line == 0) & side) | ((line == 1) & ~side), FAR, 0.0)
        key_side = jnp.where(wrap_ref[0] > 0, key_side, 0.0)
        for h in range(heads):
            query_x[h, head_width:, :] = query_side.astype(BF16)
            key_x[h, head_width:, :] = key_side.astype(BF16)

    count = probs_ref.shape[0]
    mine = pl.ds(step * count, count)
    attend(key_x.at[mine], query_x.at[mine], values_ref.at[mine], probs_ref, attended_ref, step)


def forward_last_kernel(
    shift_ref,
    first_rows,
    second_rows,
    top_ref,
    bottom_ref,
    out_ref,
    query_x,
    key_x,
    value_ref,
    first_ref,
    probs_ref,
    attended_ref,
    block_first,
    block_second,
):
    step = pl.program_id(0)
    length, width = 2 * top_ref.shape[0], top_ref.shape[1]
    attend(key_x, query_x, value_ref, probs_ref, attended_ref, step)

    @pl.when(step == pl.num_programs(0) - 1)
    def _():
        rows = joined(shift_ref[0], first_rows, second_rows, top_ref, bottom_ref)
        attended = jnp.concatenate(
            [r[...].reshape(width // 2, length) for r in (first_ref, attended_ref)], axis=0
        )
        added = nn(jnp.transpose(out_ref[...]), attended)
        block = (rows.astype(F32) + jnp.transpose(added)).astype(BF16)
        block_first[...] = block[: length // 2]
        block_second[...] = block[length // 2 :]


def per_step(shape, first):
    return pl.BlockSpec(shape, lambda i: (i + first, 0, 0))


def forward(shift, wrap, pair, weights):
    half, width = pair[0].shape
    length = 2 * half
    head_width = width // HEADS
    some = HEADS // 2
    count = FORWARD_HEADS
    extended = (HEADS, head_width + 16, length)
    split = (HEADS, head_width, length)
    first_split = (some, head_width, length)
    rows_specs = [whole((half, width))] * 4
    probs_a, hidden, normed, inverse, query_x, key_x, values, attended_a = pl.pallas_call(
        forward_first_kernel,
        grid=(some // count,),
        in_specs=[SMEM, SMEM]
        + rows_specs
        + [
            pl.BlockSpec((width, 3 * width), lambda h: (0, 0)),
            pl.BlockSpec((width, GAIN_COLS), lambda h: (0, 4 * width // GAIN_COLS)),
        ],
        out_specs=[
            per_step((count, length, length), 0),
            whole((width, length)),
            whole((width, length)),
            whole((1, length)),
            whole(extended),
            whole(extended),
            whole(split),
            whole(first_split),
        ],
        out_shape=[
            jax.ShapeDtypeStruct((some, length, length), PROBS),
            jax.ShapeDtypeStruct((width, length), BF16),
            jax.ShapeDtypeStruct((width, length), F32),
            jax.ShapeDtypeStruct((1, length), F32),
            jax.ShapeDtypeStruct(extended, BF16),
            jax.ShapeDtypeStruct(extended, BF16),
            jax.ShapeDtypeStruct(split, BF16),
            jax.ShapeDtypeStruct(first_split, BF16),
        ],
        compiler_params=params(),
        cost_estimate=lasting(25),
        name="forward_first",
    )(shift, wrap, *pair, weights, weights)
    skip = some // count
    probs_b, attended_b, *block = pl.pallas_call(
        forward_last_kernel,
        grid=(some // count,),
        in_specs=[SMEM]
        + rows_specs
        + [
            pl.BlockSpec((width, width), lambda h: (0, 3)),
            per_step((count,) + extended[1:], skip),
            per_step((count,) + extended[1:], skip),
            per_step((count,) + split[1:], skip),
            whole(first_split),
        ],
        out_specs=[
            per_step((count, length, length), 0),
            whole(first_split),
            whole((half, width)),
            whole((half, width)),
        ],
        out_shape=[
            jax.ShapeDtypeStruct((some, length, length), PROBS),
            jax.ShapeDtypeStruct(first_split, BF16),
            jax.ShapeDtypeStruct((half, width), BF16),
            jax.ShapeDtypeStruct((half, width), BF16),
        ],
        compiler_params=params(),
        cost_estimate=lasting(20),
        name="forward_last",
    )(shift, *pair, weights, query_x, key_x, values, attended_a)
    return block, (probs_a, probs_b), (query_x, key_x, values), (attended_a, attended_b), (
        hidden,
        normed,
        inverse,
    )


def attend_back(probs_ref, query_x, key_x, values_ref, attended_ref, upstream_ref, grads_ref, step):
    heads, head_width, length = values_ref.shape
    scale = head_width ** (-0.5)
    for h in range(heads):
        query, key, value = query_x[h, :head_width, :], key_x[h, :head_width, :], values_ref[h]
        upstream = upstream_ref[h]
        value_rows = jnp.transpose(value)
        offset = jnp.sum(
            upstream.astype(F32) * attended_ref[h].astype(F32), axis=0, keepdims=True
        )
        head = step * heads + h
        key_grad = value_grad = 0.0
        for start in range(0, length, BACKWARD_CHUNK):
            cols = slice(start, start + BACKWARD_CHUNK)
            probs = probs_ref[h, :, cols]
            along = nn(value_rows, upstream[:, cols])
            slopes = (probs.astype(F32) * (along - offset[:, cols]) * scale).astype(BF16)
            grads_ref[0, head, :, cols] = nn(key, slopes).astype(BF16)
            key_grad = key_grad + nt(query[:, cols], slopes)
            value_grad = value_grad + nt(upstream[:, cols], probs.astype(BF16))
        grads_ref[1, head] = key_grad.astype(BF16)
        grads_ref[2, head] = value_grad.astype(BF16)


def backward_first_kernel(
    shift_ref,
    first_rows,
    second_rows,
    top_ref,
    bottom_ref,
    out_ref,
    probs_ref,
    query_x,
    key_x,
    values_ref,
    attended_ref,
    hidden_ref,
    attended_a_ref,
    attended_b_ref,
    core_ref,
    cot_ref,
    upstream_b_ref,
    grads_ref,
    keep_ref,
    send_ref,
    upstream_a,
):
    step = pl.program_id(0)
    some, head_width, length = upstream_a.shape
    count = probs_ref.shape[0]

    @pl.when(step == 0)
    def _():
        rows = joined(shift_ref[0], first_rows, second_rows, top_ref, bottom_ref)
        cot_ref[...] = rows
        upstream = nt(out_ref[...], rows).astype(BF16).reshape(2, some, head_width, length)
        upstream_a[...] = upstream[0]
        upstream_b_ref[...] = upstream[1]

    attend_back(
        probs_ref,
        query_x,
        key_x,
        values_ref,
        attended_ref,
        upstream_a.at[pl.ds(step * count, count)],
        grads_ref,
        step,
    )

    @pl.when(step == pl.num_programs(0) - 1)
    def _():
        width = cot_ref.shape[1]
        part_in = nt(hidden_ref[...], grads_ref[...].reshape(3 * width // 2, length))
        part_out = [
            nn(out[...].reshape(width // 2, length), cot_ref[...])
            for out in (attended_a_ref, attended_b_ref)
        ]
        parts = jnp.concatenate([part_in, jnp.concatenate(part_out, axis=0)], axis=1)
        keep_and_send(core_ref[0], parts, keep_ref, send_ref)


def keep_and_send(core, parts, keep_ref, send_ref):
    half = parts.shape[1] // 2
    first, second = parts[:, :half], parts[:, half:]
    keep_ref[...] = jnp.where(core == 0, first, second)
    send_ref[...] = jnp.where(core == 0, second, first)


def backward_last_kernel(
    in_ref,
    gain_ref,
    probs_ref,
    hidden_ref,
    normed_ref,
    inverse_ref,
    query_x,
    key_x,
    values_ref,
    attended_ref,
    upstream_ref,
    first_ref,
    cot_ref,
    core_ref,
    *refs,
):
    grad_first, grad_second, keep_ref, send_ref, gain_out, grads = refs[-6:]
    step = pl.program_id(0)
    length, width = cot_ref.shape
    half = width // 2
    attend_back(
        probs_ref, query_x, key_x, values_ref, attended_ref, upstream_ref, grads, step
    )

    @pl.when(step == pl.num_programs(0) - 1)
    def _():
        grad_hidden = 0.0
        for group, ref in enumerate((first_ref, grads)):
            for part in range(3):
                first = part * width + group * half
                grad_hidden = grad_hidden + nn(
                    in_ref[:, first : first + half], ref[part].reshape(half, length)
                )
        parts = nt(hidden_ref[...], grads[...].reshape(3 * half, length))
        keep_and_send(core_ref[0], parts, keep_ref, send_ref)
        normed = normed_ref[...]
        part_gain = jnp.sum(grad_hidden * normed, axis=1, keepdims=True)
        part_gain = jnp.transpose(jnp.broadcast_to(part_gain, (width, LANES)))[:1, :]
        lines = [part_gain[:, start : start + LANES] for start in range(0, width, LANES)]
        lines.append(jnp.zeros((8 - len(lines), LANES), F32))
        gain_out[...] = jnp.concatenate(lines, axis=0)
        scaled = grad_hidden * gain_ref[:, :1].astype(F32)
        middle = jnp.mean(scaled, axis=0, keepdims=True)
        slope = jnp.mean(scaled * normed, axis=0, keepdims=True)
        change = inverse_ref[...] * (scaled - middle - normed * slope)
        grad = (cot_ref[...].astype(F32) + jnp.transpose(change)).astype(BF16)
        grad_first[...] = grad[: length // 2]
        grad_second[...] = grad[length // 2 :]


def backward_first(shift, pair, weights, probs, split, attended, hidden, core):
    half, width = pair[0].shape
    length = 2 * half
    head_width = width // HEADS
    some = HEADS // 2
    count = BACKWARD_HEADS
    group = (some, head_width, length)
    extended = (count, head_width + 16, length)
    return pl.pallas_call(
        backward_first_kernel,
        grid=(some // count,),
        in_specs=[
            SMEM,
            whole((half, width)),
            whole((half, width)),
            whole((half, width)),
            whole((half, width)),
            pl.BlockSpec((width, width), lambda h: (0, 3)),
            per_step((count, length, length), 0),
            per_step(extended, 0),
            per_step(extended, 0),
            per_step((count, head_width, length), 0),
            per_step((count, head_width, length), 0),
            whole((width, length)),
            whole(group),
            whole(group),
            SMEM,
        ],
        out_specs=[
            whole((length, width)),
            whole(group),
            whole((3,) + group),
            whole((width, 5 * width // 4)),
            whole((width, 5 * width // 4)),
        ],
        out_shape=[
            jax.ShapeDtypeStruct((length, width), BF16),
            jax.ShapeDtypeStruct(group, BF16),
            jax.ShapeDtypeStruct((3,) + group, BF16),
            jax.ShapeDtypeStruct((width, 5 * width // 4), F32),
            jax.ShapeDtypeStruct((width, 5 * width // 4), F32),
        ],
        scratch_shapes=[pltpu.VMEM(group, BF16)],
        compiler_params=params(),
        cost_estimate=lasting(25),
        name="backward_first",
    )(shift, *pair, weights, probs, *split, attended[0], hidden, *attended, core)


def backward_last(weights, probs, rows, split, attended, upstream, first, cot, core, after):
    length, width = cot.shape
    head_width = width // HEADS
    some = HEADS // 2
    count = BACKWARD_HEADS
    skip = some // count
    group = (some, head_width, length)
    extended = (count, head_width + 16, length)
    one = (count, head_width, length)
    return pl.pallas_call(
        backward_last_kernel,
        grid=(some // count,),
        in_specs=[
            pl.BlockSpec((width, 3 * width), lambda h: (0, 0)),
            pl.BlockSpec((width, GAIN_COLS), lambda h: (0, 4 * width // GAIN_COLS)),
            per_step((count, length, length), 0),
            whole((width, length)),
            whole((width, length)),
            whole((1, length)),
            per_step(extended, skip),
            per_step(extended, skip),
            per_step(one, skip),
            per_step(one, 0),
            per_step(one, 0),
            whole((3,) + group),
            whole((length, width)),
            SMEM,
        ]
        + [ANY] * len(after),
        out_specs=[
            whole((length // 2, width)),
            whole((length // 2, width)),
            whole((width, 3 * width // 4)),
            whole((width, 3 * width // 4)),
            whole((8, LANES)),
        ],
        out_shape=[
            jax.ShapeDtypeStruct((length // 2, width), BF16),
            jax.ShapeDtypeStruct((length // 2, width), BF16),
            jax.ShapeDtypeStruct((width, 3 * width // 4), F32),
            jax.ShapeDtypeStruct((width, 3 * width // 4), F32),
            jax.ShapeDtypeStruct((8, LANES), F32),
        ],
        scratch_shapes=[pltpu.VMEM((3,) + group, BF16)],
        compiler_params=params(),
        cost_estimate=lasting(25),
        name="backward_last",
    )(
        weights,
        weights,
        probs,
        *rows,
        *split,
        attended[1],
        upstream,
        first,
        cot,
        core,
        *after,
    )


def exchange(rows, devices):
    moved = lax.all_to_all(
        rows.reshape(devices, rows.shape[0] // devices, rows.shape[1]),
        BOTH,
        split_axis=0,
        concat_axis=0,
        tiled=True,
    )
    return moved.reshape(rows.shape)


def with_neighbours(first, second):
    devices = lax.axis_size(BOTH)
    ahead = [(seat(i), seat((i + 1) % devices)) for i in range(devices)]
    behind = [(j, i) for i, j in ahead]
    return first, second, lax.ppermute(first, BOTH, ahead), lax.ppermute(second, BOTH, behind)


def with_neighbours_back(first, second):
    devices = lax.axis_size(BOTH)
    ahead = [(seat(i), seat((i + 1) % devices)) for i in range(devices)]
    behind = [(j, i) for i, j in ahead]
    return first, second, lax.ppermute(first, BOTH, behind), lax.ppermute(second, BOTH, ahead)


def other_core(array):
    pairs = [(i, i ^ 1) for i in range(lax.axis_size("fsdp"))]
    return lax.ppermute(array, "fsdp", pairs)


def over_chips(terms):
    count, far = lax.axis_size("fsdp"), 2
    while far < count:
        terms = terms + lax.ppermute(terms, "fsdp", [(i, i ^ far) for i in range(count)])
        far *= 2
    return terms


def curve_work(shift_offset, got_points, send_cot, weights):
    devices, groups = lax.axis_size(BOTH), lax.axis_size("dp")
    width, share = send_cot.shape[1], weights.shape[0] // lax.axis_size("fsdp")
    edge_device = jnp.where(2 * shift_offset <= PATCH, seat(devices - 1), seat(0))
    wrap = (lax.axis_index(BOTH) == edge_device).astype(jnp.int32)
    core = (lax.axis_index("fsdp") % 2).astype(jnp.int32).reshape(1)

    *own_points, place = land_first(shift_offset, got_points, width, (send_cot,))
    points_pair = with_neighbours(*own_points)
    got_cot = exchange(send_cot, devices)
    block, (probs_a, probs_b), split, attended, (hidden, normed, inverse) = forward(
        shift_offset, wrap, points_pair, weights
    )
    cot_pair = with_neighbours(*land_second(place, got_cot, (probs_a,)))
    block_pair = with_neighbours_back(*block)

    cot, upstream, first_grads, first_keep, first_send = backward_first(
        shift_offset, cot_pair, weights, probs_a, split, attended, hidden, core
    )
    spread_block = spread_pair(shift_offset, place, block_pair, "back_block", after=(first_grads,))
    back_block = exchange(spread_block, devices)
    *grad, last_keep, last_send, part_gain = backward_last(
        weights,
        probs_b,
        (hidden, normed, inverse),
        split,
        attended,
        upstream,
        first_grads,
        cot,
        core,
        (spread_block,),
    )
    grad_pair = with_neighbours_back(*grad)
    parts = (first_keep, other_core(first_send), last_keep, other_core(last_send))
    gain_terms = over_chips(part_gain)
    spread_grad = spread_pair(
        shift_offset, place, grad_pair, "back_grad", parts, (groups, share), (back_block, gain_terms)
    )
    return spread_grad, back_block, gain_terms + other_core(gain_terms)


def body(
    points,
    cotangent,
    destination,
    curve_slot,
    point_counts,
    shift_offset,
    project_in,
    project_out,
    norm_gain,
):
    devices, groups = lax.axis_size(BOTH), lax.axis_size("dp")
    arrived, width = points.shape
    share = project_in.shape[0]
    packed = pack(project_in, project_out, norm_gain)
    weights = lax.all_gather(packed, "fsdp", axis=0, tiled=True)
    send_points, target = send_first(
        shift_offset,
        point_counts,
        destination.reshape(1, arrived),
        curve_slot.reshape(1, arrived),
        points,
        devices,
        (packed,),
    )
    got_points = exchange(send_points, devices)
    send_cot = pick(target, cotangent, arrived, "send_cot")
    spread_grad, back_block, gain_terms = curve_work(shift_offset, got_points, send_cot, weights)
    back_grad = exchange(spread_grad, devices)
    block_out = spread(target, back_block, width, "block_out", (spread_grad,))
    sums = add_tiles(back_grad, gain_terms, width, groups, (block_out,))
    tiles = lax.all_to_all(sums, "dp", split_axis=0, concat_axis=0, tiled=True)
    point_grad = spread(target, back_grad, width, "point_grad", (sums,))
    columns = (5 * width // 4, 3 * width // 4)
    member = lax.axis_index("fsdp").astype(jnp.int32).reshape(1)
    grad_in, grad_out, grad_gain = settle(member, tiles, (groups, share), columns, width)
    return block_out, point_grad, grad_in, grad_out, grad_gain.reshape(share)


def solution(mesh):
    in_specs = (
        P(BOTH, None),
        P(BOTH, None),
        P(BOTH),
        P(BOTH),
        P(BOTH),
        P(),
        P("fsdp", None),
        P("fsdp", None),
        P("fsdp"),
    )
    out_specs = (
        P(BOTH, None),
        P(BOTH, None),
        P("fsdp", None),
        P("fsdp", None),
        P("fsdp"),
    )
    return jax.shard_map(body, mesh=mesh, in_specs=in_specs, out_specs=out_specs, check_vma=False)
```

```python
import functools

import jax
import jax.numpy as jnp
from jax import lax
from jax.experimental import pallas as pl
from jax.experimental.pallas import tpu as pltpu
from jax.sharding import PartitionSpec as P

HEADS = 16
PATCH = 1024
EPS = 1e-05
BOTH = ("dp", "fsdp")
GAIN_COLS = 128
MARK_COLS = 128
LANES = 128
TILE_ROWS = 16
FAR = -1e30
LOG2E = 1.4426950408889634
F32 = jnp.float32
BF16 = jnp.bfloat16
FORWARD_HEADS, FORWARD_CHUNK = 2, 1024
BACKWARD_HEADS, BACKWARD_CHUNK = 1, 512
PROBS = F32
VMEM_BYTES = 63 * 1024 * 1024


def params(steps=1):
    return pltpu.CompilerParams(
        vmem_limit_bytes=VMEM_BYTES, dimension_semantics=("arbitrary",) * steps
    )


def whole(shape):
    zeros = (0,) * len(shape)
    return pl.BlockSpec(shape, lambda *_: zeros)


SMEM = pl.BlockSpec(memory_space=pltpu.SMEM)
ANY = pl.BlockSpec(memory_space=pl.ANY)


def lasting(us):
    return pl.CostEstimate(flops=int(us * 1e9), bytes_accessed=0, transcendentals=0)


def ones_where(mask, dtype=BF16):
    return jnp.where(mask, 1.0, 0.0).astype(dtype)


def iota(shape, dim):
    return lax.broadcasted_iota(jnp.int32, shape, dim)


def nt(a, b):
    return lax.dot_general(a, b, (((1,), (1,)), ((), ())), preferred_element_type=F32)


def nn(a, b):
    return jnp.dot(a, b, preferred_element_type=F32)


def pick_rows(index_row, rows, first, count):
    slots = index_row.shape[1]
    chosen = ones_where(iota((count, slots), 0) + first == index_row)
    return nn(chosen, rows).astype(BF16)


def seat(shard):
    core, along_y = shard & 1, (shard >> 1) & 3
    along_z, along_x = (shard >> 3) & 3, shard >> 5
    y, z = (along_y - along_z) & 3, (along_z - along_x) & 3
    return (((along_x << 2) + z << 2) + y << 1) + core


def slot_targets(count, dest_ref, target_ref, devices):
    arrived = dest_ref.shape[1]
    capacity = arrived // devices
    chunk = 256
    before = ones_where(iota((chunk, chunk), 0) < iota((chunk, chunk), 1))
    base = jnp.zeros((devices, 1), F32)
    for start in range(0, arrived, chunk):
        cols = pl.ds(start, chunk)
        dest = seat(dest_ref[:, cols])
        valid = iota((1, chunk), 1) + start < count
        here = jnp.where((iota((devices, chunk), 0) == dest) & valid, 1.0, 0.0)
        ahead = nn(here.astype(BF16), before) + base
        rank = jnp.sum(here * ahead, axis=0, keepdims=True).astype(jnp.int32)
        base = base + jnp.sum(here, axis=1, keepdims=True)
        target_ref[:, cols] = jnp.where(valid, dest * capacity + rank, -1)


def send_first_kernel(devices, shift_ref, count_ref, dest_ref, slot_ref, rows_ref, *refs):
    send_ref, target_ref = refs[-2:]
    step = pl.program_id(0)

    @pl.when(step == 0)
    def _():
        slot_targets(count_ref[0], dest_ref, target_ref, devices)

    block = send_ref.shape[0]
    arrived, width = rows_ref.shape
    chosen = ones_where(iota((block, arrived), 0) + step * block == target_ref[...])
    send_ref[:, :width] = nn(chosen, rows_ref[...]).astype(BF16)
    code = jnp.where(slot_ref[...] < shift_ref[0], 2.0, 1.0)
    send_ref[:, width:] = nt(chosen, jnp.broadcast_to(code, (MARK_COLS, arrived)).astype(BF16)).astype(BF16)


def send_first(shift, count, dest, slot, rows, devices, after, block=512):
    arrived, width = rows.shape
    wide = width + MARK_COLS
    return pl.pallas_call(
        functools.partial(send_first_kernel, devices),
        grid=(arrived // block,),
        in_specs=[SMEM, SMEM, whole((1, arrived)), whole((1, arrived)), whole((arrived, width))]
        + [ANY] * len(after),
        out_specs=[pl.BlockSpec((block, wide), lambda i: (i, 0)), whole((1, arrived))],
        out_shape=[
            jax.ShapeDtypeStruct((arrived, wide), BF16),
            jax.ShapeDtypeStruct((1, arrived), jnp.int32),
        ],
        compiler_params=params(),
        cost_estimate=lasting(9),
        name="send_points",
    )(shift, count, dest, slot, rows, *after)


def pick_kernel(index_ref, rows_ref, *refs):
    out_ref = refs[-1]
    block = out_ref.shape[0]
    out_ref[...] = pick_rows(index_ref[...], rows_ref[...], pl.program_id(0) * block, block)


def pick(index, rows, out_rows, name, after=(), block=512):
    arrived, width = rows.shape
    return pl.pallas_call(
        pick_kernel,
        grid=(out_rows // block,),
        in_specs=[whole((1, arrived)), whole((arrived, width))] + [ANY] * len(after),
        out_specs=pl.BlockSpec((block, width), lambda i: (i, 0)),
        out_shape=jax.ShapeDtypeStruct((out_rows, width), BF16),
        compiler_params=params(),
        cost_estimate=lasting(8),
        name=name,
    )(index, rows, *after)


def places(shift, marks_ref, place_ref):
    slots = marks_ref.shape[0]
    marks = jnp.transpose(marks_ref[...].astype(F32))[:1, :]
    chunk = 256
    before = ones_where(iota((chunk, chunk), 0) < iota((chunk, chunk), 1))
    line = iota((8, 1), 0)
    first = lax.convert_element_type(PATCH - shift, F32)
    base = jnp.where(line == 1, first, 0.0)
    for start in range(0, slots, chunk):
        here = marks[:, start : start + chunk]
        flags = jnp.where(here == (line + 1).astype(F32), 1.0, 0.0)
        flags = jnp.where(line < 2, flags, 0.0)
        earlier = nn(flags.astype(BF16), before) + base
        base = base + jnp.sum(flags, axis=1, keepdims=True)
        place = jnp.sum(flags * earlier, axis=0, keepdims=True).astype(jnp.int32)
        place_ref[:, start : start + chunk] = jnp.where(here > 0.0, place, -1)


def halves_out(first, second, index_row, rows):
    half = first.shape[0]
    first[...] = pick_rows(index_row, rows, 0, half)
    second[...] = pick_rows(index_row, rows, half, half)


def land_first_kernel(shift_ref, marks_ref, rows_ref, *refs):
    first_ref, second_ref, place_ref = refs[-3:]
    places(shift_ref[0], marks_ref, place_ref)
    halves_out(first_ref, second_ref, place_ref[...], rows_ref[...])


def land_first(shift, got, width, after):
    slots, wide = got.shape
    half = PATCH // 2
    return pl.pallas_call(
        land_first_kernel,
        grid=(1,),
        in_specs=[
            SMEM,
            pl.BlockSpec((slots, MARK_COLS), lambda i: (0, width // MARK_COLS)),
            pl.BlockSpec((slots, width), lambda i: (0, 0)),
        ]
        + [ANY] * len(after),
        out_specs=[whole((half, width)), whole((half, width)), whole((1, slots))],
        out_shape=[
            jax.ShapeDtypeStruct((half, width), BF16),
            jax.ShapeDtypeStruct((half, width), BF16),
            jax.ShapeDtypeStruct((1, slots), jnp.int32),
        ],
        compiler_params=params(),
        cost_estimate=lasting(7),
        name="land_points",
    )(shift, got, got, *after)


def land_second_kernel(place_ref, rows_ref, *refs):
    first_ref, second_ref = refs[-2:]
    halves_out(first_ref, second_ref, place_ref[...], rows_ref[...])


def land_second(place, got, after):
    slots, width = got.shape
    half = PATCH // 2
    return pl.pallas_call(
        land_second_kernel,
        grid=(1,),
        in_specs=[whole((1, slots)), whole((slots, width))] + [ANY] * len(after),
        out_specs=[whole((half, width)), whole((half, width))],
        out_shape=[jax.ShapeDtypeStruct((half, width), BF16)] * 2,
        compiler_params=params(),
        cost_estimate=lasting(5),
        name="land_cot",
    )(place, got, *after)


def pack_kernel(in_ref, out_ref, gain_ref, packed_ref):
    inner, outer = in_ref.shape[1], out_ref.shape[1]
    packed_ref[:, :inner] = in_ref[...]
    packed_ref[:, inner : inner + outer] = out_ref[...]
    column = jnp.transpose(jnp.broadcast_to(gain_ref[...].astype(F32), (GAIN_COLS, gain_ref.shape[1])))
    packed_ref[:, inner + outer :] = column.astype(BF16)


def pack(project_in, project_out, gain):
    share = project_in.shape[0]
    columns = project_in.shape[1] + project_out.shape[1] + GAIN_COLS
    return pl.pallas_call(
        pack_kernel,
        grid=(1,),
        in_specs=[whole(project_in.shape), whole(project_out.shape), whole((1, share))],
        out_specs=whole((share, columns)),
        out_shape=jax.ShapeDtypeStruct((share, columns), BF16),
        compiler_params=params(),
        cost_estimate=lasting(1),
        name="pack_weights",
    )(project_in, project_out, gain.reshape(1, share))


def column_of(row):
    length = row.shape[1]
    return jnp.transpose(jnp.broadcast_to(row, (128, length)))


def spread_rows(index_row, rows):
    wide = column_of(index_row)
    count = wide.shape[0]
    lanes = iota((count, 128), 1)
    chosen = jnp.concatenate(
        [ones_where(wide == lanes + start) for start in range(0, rows.shape[0], 128)], axis=1
    )
    return nn(chosen, rows).astype(BF16)


def spread_kernel(index_ref, rows_ref, *refs):
    out_ref = refs[-1]
    out_ref[...] = spread_rows(index_ref[...], rows_ref[...])


def spread(index, rows, width, name, after=(), block=512):
    slots, source = index.shape[1], rows.shape[0]
    return pl.pallas_call(
        spread_kernel,
        grid=(slots // block,),
        in_specs=[pl.BlockSpec((1, block), lambda i: (0, i)), whole((source, width))]
        + [ANY] * len(after),
        out_specs=pl.BlockSpec((block, width), lambda i: (i, 0)),
        out_shape=jax.ShapeDtypeStruct((slots, width), BF16),
        compiler_params=params(),
        cost_estimate=lasting(8),
        name=name,
    )(index, rows, *after)


def spread_pair_kernel(groups, shift_ref, index_ref, first_rows, second_rows, top_ref, bottom_ref, *refs):
    out_ref, rows = refs[-2:]
    step = pl.program_id(0)

    @pl.when(step == 0)
    def _():
        rows[...] = joined(shift_ref[0], first_rows, second_rows, top_ref, bottom_ref)

    width = rows.shape[1]
    out_ref[:, :width] = spread_rows(index_ref[...], rows[...])
    if groups is None:
        return
    shares, of_rows = groups
    across = shares * TILE_ROWS // of_rows
    members = refs[0].shape[0] // of_rows
    blocks = [
        (keep, got, pl.ds(start, LANES))
        for keep, got in (refs[0:2], refs[2:4])
        for start in range(0, keep.shape[1], LANES)
    ]
    for number, (keep, got, lanes) in enumerate(blocks):
        start = width + number // across * LANES
        for f in range(members):
            source = pl.ds(pl.multiple_of(f * of_rows + step * TILE_ROWS, TILE_ROWS), TILE_ROWS)
            to = (number % across * members + f) * TILE_ROWS
            out_ref[to : to + TILE_ROWS, start : start + LANES] = (
                keep[source, lanes] + got[source, lanes]
            ).astype(BF16)


def spread_pair(shift, index, pair, name, parts=(), groups=None, after=()):
    slots = index.shape[1]
    half, width = pair[0].shape
    blocks = groups[1] // TILE_ROWS if parts else 4
    wide = width + sum(part.shape[1] for part in parts[::2]) * LANES // width
    block = slots // blocks
    return pl.pallas_call(
        functools.partial(spread_pair_kernel, groups),
        grid=(blocks,),
        in_specs=[SMEM, pl.BlockSpec((1, block), lambda i: (0, i))]
        + [whole((half, width))] * 4
        + [whole(part.shape) for part in parts]
        + [ANY] * len(after),
        out_specs=pl.BlockSpec((block, wide), lambda i: (i, 0)),
        out_shape=jax.ShapeDtypeStruct((slots, wide), BF16),
        scratch_shapes=[pltpu.VMEM((2 * half, width), BF16)],
        compiler_params=params(),
        cost_estimate=lasting(6),
        name=name,
    )(shift, index, *pair, *parts, *after)


def add_tiles_kernel(tiles_ref, gain_ref, *refs):
    out_ref = refs[-1]
    slots, lanes = tiles_ref.shape
    pairs = tiles_ref[...].astype(F32).reshape(slots // TILE_ROWS // 2, 2, TILE_ROWS, lanes)
    sums = jnp.sum(pairs, axis=0)
    gain = jnp.concatenate([gain_ref[...], jnp.zeros((TILE_ROWS - 8, LANES), F32)], axis=0)
    line = jnp.concatenate([sums[0], sums[1], gain], axis=1)
    out_ref[...] = jnp.broadcast_to(line[None], out_ref.shape)


def add_tiles(got, gain, width, shares, after):
    slots, wide = got.shape
    more = wide - width
    shape = (shares, TILE_ROWS, 2 * more + LANES)
    return pl.pallas_call(
        add_tiles_kernel,
        grid=(1,),
        in_specs=[pl.BlockSpec((slots, more), lambda i: (0, width // more)), whole(gain.shape)]
        + [ANY] * len(after),
        out_specs=whole(shape),
        out_shape=jax.ShapeDtypeStruct(shape, F32),
        compiler_params=params(),
        cost_estimate=lasting(2),
        name="add_tiles",
    )(got, gain, *after)


def settle_kernel(groups, columns, member_ref, tiles_ref, in_ref, out_ref, gain_ref):
    shares, of_rows = groups
    across = shares * TILE_ROWS // of_rows
    width = out_ref.shape[1]
    half = width // 2
    each = (tiles_ref.shape[2] - LANES) // LANES // 2
    for share in range(shares):
        rows = pl.ds(share // across * TILE_ROWS, TILE_ROWS)
        for core in range(2):
            for k in range(each):
                lane = (core * each + k) * LANES
                tile = tiles_ref[share, :, lane : lane + LANES]
                column = (k * across + share % across) * LANES
                group = column // columns[0]
                column = column - group * columns[0] + core * columns[group]
                part, start = column // half, column % half
                if part < 3:
                    start += part * width + group * half
                    in_ref[rows, start : start + LANES] = tile
                else:
                    start = column - 3 * half
                    out_ref[rows, start : start + LANES] = tile
    gains = jnp.sum(tiles_ref[:, :8, 2 * each * LANES :], axis=0)
    a_line = LANES // of_rows
    mine = iota(gains.shape, 0) == lax.div(member_ref[0], a_line)
    line = jnp.sum(jnp.where(mine, gains, 0.0), axis=0, keepdims=True)
    gain_ref[...] = line[:, :of_rows]
    for piece in range(1, a_line):
        @pl.when(lax.rem(member_ref[0], a_line) == piece)
        def _():
            gain_ref[...] = line[:, piece * of_rows : (piece + 1) * of_rows]


def settle(member, tiles, groups, columns, width):
    of_rows = groups[1]
    shapes = [(of_rows, 3 * width), (of_rows, width), (1, of_rows)]
    return pl.pallas_call(
        functools.partial(settle_kernel, groups, columns),
        grid=(1,),
        in_specs=[SMEM, whole(tiles.shape)],
        out_specs=[whole(shape) for shape in shapes],
        out_shape=[jax.ShapeDtypeStruct(shape, F32) for shape in shapes],
        compiler_params=params(),
        cost_estimate=lasting(2),
        name="settle",
    )(member, tiles)


def turn_kernel(in_ref, out_ref, *refs):
    turned_ref = refs[-1]
    width = out_ref.shape[0]
    for part in range(3):
        columns = slice(part * width, (part + 1) * width)
        turned_ref[columns, :] = jnp.transpose(in_ref[:, columns])
    turned_ref[3 * width :, :] = jnp.transpose(out_ref[...])


def turn(weights, width, after):
    return pl.pallas_call(
        turn_kernel,
        grid=(1,),
        in_specs=[
            pl.BlockSpec((width, 3 * width), lambda i: (0, 0)),
            pl.BlockSpec((width, width), lambda i: (0, 3)),
        ]
        + [ANY] * len(after),
        out_specs=whole((4 * width, width)),
        out_shape=jax.ShapeDtypeStruct((4 * width, width), BF16),
        compiler_params=params(),
        cost_estimate=lasting(2),
        name="turn_weights",
    )(weights, weights, *after)


def gate_kernel(*refs):
    pass


def gate(array, *after):
    return pl.pallas_call(
        gate_kernel,
        in_specs=[ANY] * (1 + len(after)),
        out_specs=ANY,
        out_shape=jax.ShapeDtypeStruct(array.shape, array.dtype),
        input_output_aliases={0: 0},
        compiler_params=pltpu.CompilerParams(has_side_effects=True),
        name="gate",
    )(array, *after)


def joined(shift, first_ref, second_ref, top_ref, bottom_ref):
    half, width = top_ref.shape
    edge = PATCH - shift
    row = iota((half, width), 0)
    first = jnp.where((2 * shift > PATCH) & (row < edge), top_ref[...], first_ref[...])
    second = jnp.where((2 * shift <= PATCH) & (row + half >= edge), bottom_ref[...], second_ref[...])
    return jnp.concatenate([first, second], axis=0)


def attend(key_x, query_x, value, probs_ref, out_ref, step):
    heads, head_width, length = value.shape
    scale = head_width ** (-0.5) * LOG2E
    for start in range(0, length, FORWARD_CHUNK):
        cols = pl.ds(start, FORWARD_CHUNK)
        scores = [nn(jnp.transpose(key_x[h]), query_x[h, :, cols]) for h in range(heads)]
        for h in range(heads):
            top = jnp.max(scores[h], axis=0, keepdims=True)
            weights = jnp.exp2((scores[h] - top) * scale)
            probs = weights * (1.0 / jnp.sum(weights, axis=0, keepdims=True))
            rounded = probs.astype(BF16)
            probs_ref[h, :, cols] = probs.astype(PROBS)
            out_ref[step * heads + h, :, cols] = nn(value[h], rounded).astype(BF16)


def forward_first_kernel(
    shift_ref,
    wrap_ref,
    first_rows,
    second_rows,
    top_ref,
    bottom_ref,
    in_ref,
    gain_ref,
    probs_ref,
    hidden_ref,
    normed_ref,
    inverse_ref,
    query_x,
    key_x,
    values_ref,
    attended_ref,
):
    step = pl.program_id(0)
    heads, head_width, length = values_ref.shape
    width = heads * head_width
    extra = query_x.shape[1] - head_width

    @pl.when(step == 0)
    def _():
        rows = joined(shift_ref[0], first_rows, second_rows, top_ref, bottom_ref)
        values_in = jnp.transpose(rows.astype(F32))
        center = values_in - jnp.mean(values_in, axis=0, keepdims=True)
        inverse = lax.rsqrt(jnp.mean(center * center, axis=0, keepdims=True) + EPS)
        normed = center * inverse
        normed_ref[...] = normed
        inverse_ref[...] = inverse
        hidden = (normed * gain_ref[:, :1].astype(F32)).astype(BF16)
        hidden_ref[...] = hidden
        for part, ref in enumerate((query_x, key_x, values_ref)):
            made = nn(in_ref[part * width : (part + 1) * width, :], hidden).astype(BF16)
            ref[:, :head_width, :] = made.reshape(heads, head_width, length)
        side = iota((extra, length), 1) >= PATCH - shift_ref[0]
        line = iota((extra, length), 0)
        query_side = jnp.where(((line == 0) & ~side) | ((line == 1) & side), 1.0, 0.0)
        key_side = jnp.where(((line == 0) & side) | ((line == 1) & ~side), FAR, 0.0)
        key_side = jnp.where(wrap_ref[0] > 0, key_side, 0.0)
        for h in range(heads):
            query_x[h, head_width:, :] = query_side.astype(BF16)
            key_x[h, head_width:, :] = key_side.astype(BF16)

    count = probs_ref.shape[0]
    mine = pl.ds(step * count, count)
    attend(key_x.at[mine], query_x.at[mine], values_ref.at[mine], probs_ref, attended_ref, step)


def forward_last_kernel(
    shift_ref,
    first_rows,
    second_rows,
    top_ref,
    bottom_ref,
    out_ref,
    query_x,
    key_x,
    value_ref,
    first_ref,
    probs_ref,
    attended_ref,
    block_first,
    block_second,
):
    step = pl.program_id(0)
    length, width = 2 * top_ref.shape[0], top_ref.shape[1]
    attend(key_x, query_x, value_ref, probs_ref, attended_ref, step)

    @pl.when(step == pl.num_programs(0) - 1)
    def _():
        rows = joined(shift_ref[0], first_rows, second_rows, top_ref, bottom_ref)
        attended = jnp.concatenate(
            [r[...].reshape(width // 2, length) for r in (first_ref, attended_ref)], axis=0
        )
        added = nn(out_ref[...], attended)
        block = (rows.astype(F32) + jnp.transpose(added)).astype(BF16)
        block_first[...] = block[: length // 2]
        block_second[...] = block[length // 2 :]


def per_step(shape, first):
    return pl.BlockSpec(shape, lambda i: (i + first, 0, 0))


def forward(shift, wrap, pair, weights, turned):
    half, width = pair[0].shape
    length = 2 * half
    head_width = width // HEADS
    some = HEADS // 2
    count = FORWARD_HEADS
    extended = (HEADS, head_width + 16, length)
    split = (HEADS, head_width, length)
    first_split = (some, head_width, length)
    rows_specs = [whole((half, width))] * 4
    probs_a, hidden, normed, inverse, query_x, key_x, values, attended_a = pl.pallas_call(
        forward_first_kernel,
        grid=(some // count,),
        in_specs=[SMEM, SMEM]
        + rows_specs
        + [
            pl.BlockSpec((3 * width, width), lambda h: (0, 0)),
            pl.BlockSpec((width, GAIN_COLS), lambda h: (0, 4 * width // GAIN_COLS)),
        ],
        out_specs=[
            per_step((count, length, length), 0),
            whole((width, length)),
            whole((width, length)),
            whole((1, length)),
            whole(extended),
            whole(extended),
            whole(split),
            whole(first_split),
        ],
        out_shape=[
            jax.ShapeDtypeStruct((some, length, length), PROBS),
            jax.ShapeDtypeStruct((width, length), BF16),
            jax.ShapeDtypeStruct((width, length), F32),
            jax.ShapeDtypeStruct((1, length), F32),
            jax.ShapeDtypeStruct(extended, BF16),
            jax.ShapeDtypeStruct(extended, BF16),
            jax.ShapeDtypeStruct(split, BF16),
            jax.ShapeDtypeStruct(first_split, BF16),
        ],
        compiler_params=params(),
        cost_estimate=lasting(25),
        name="forward_first",
    )(shift, wrap, *pair, turned, weights)
    skip = some // count
    probs_b, attended_b, *block = pl.pallas_call(
        forward_last_kernel,
        grid=(some // count,),
        in_specs=[SMEM]
        + rows_specs
        + [
            pl.BlockSpec((width, width), lambda h: (3, 0)),
            per_step((count,) + extended[1:], skip),
            per_step((count,) + extended[1:], skip),
            per_step((count,) + split[1:], skip),
            whole(first_split),
        ],
        out_specs=[
            per_step((count, length, length), 0),
            whole(first_split),
            whole((half, width)),
            whole((half, width)),
        ],
        out_shape=[
            jax.ShapeDtypeStruct((some, length, length), PROBS),
            jax.ShapeDtypeStruct(first_split, BF16),
            jax.ShapeDtypeStruct((half, width), BF16),
            jax.ShapeDtypeStruct((half, width), BF16),
        ],
        compiler_params=params(),
        cost_estimate=lasting(20),
        name="forward_last",
    )(shift, *pair, turned, query_x, key_x, values, attended_a)
    return block, (probs_a, probs_b), (query_x, key_x, values), (attended_a, attended_b), (
        hidden,
        normed,
        inverse,
    )


def attend_back(probs_ref, query_x, key_x, values_ref, attended_ref, upstream_ref, grads_ref, step):
    heads, head_width, length = values_ref.shape
    scale = head_width ** (-0.5)
    for h in range(heads):
        query, key, value = query_x[h, :head_width, :], key_x[h, :head_width, :], values_ref[h]
        upstream = upstream_ref[h]
        value_rows = jnp.transpose(value)
        offset = jnp.sum(
            upstream.astype(F32) * attended_ref[h].astype(F32), axis=0, keepdims=True
        )
        head = step * heads + h
        key_grad = value_grad = 0.0
        for start in range(0, length, BACKWARD_CHUNK):
            cols = slice(start, start + BACKWARD_CHUNK)
            probs = probs_ref[h, :, cols]
            along = nn(value_rows, upstream[:, cols])
            slopes = (probs.astype(F32) * (along - offset[:, cols]) * scale).astype(BF16)
            grads_ref[0, head, :, cols] = nn(key, slopes).astype(BF16)
            key_grad = key_grad + nt(query[:, cols], slopes)
            value_grad = value_grad + nt(upstream[:, cols], probs.astype(BF16))
        grads_ref[1, head] = key_grad.astype(BF16)
        grads_ref[2, head] = value_grad.astype(BF16)


def backward_first_kernel(
    shift_ref,
    first_rows,
    second_rows,
    top_ref,
    bottom_ref,
    out_ref,
    probs_ref,
    query_x,
    key_x,
    values_ref,
    attended_ref,
    hidden_ref,
    attended_a_ref,
    attended_b_ref,
    core_ref,
    cot_ref,
    upstream_b_ref,
    grads_ref,
    keep_ref,
    send_ref,
    upstream_a,
):
    step = pl.program_id(0)
    some, head_width, length = upstream_a.shape
    count = probs_ref.shape[0]

    @pl.when(step == 0)
    def _():
        rows = joined(shift_ref[0], first_rows, second_rows, top_ref, bottom_ref)
        cot_ref[...] = rows
        upstream = nt(out_ref[...], rows).astype(BF16).reshape(2, some, head_width, length)
        upstream_a[...] = upstream[0]
        upstream_b_ref[...] = upstream[1]

    attend_back(
        probs_ref,
        query_x,
        key_x,
        values_ref,
        attended_ref,
        upstream_a.at[pl.ds(step * count, count)],
        grads_ref,
        step,
    )

    @pl.when(step == pl.num_programs(0) - 1)
    def _():
        width = cot_ref.shape[1]
        part_in = nt(hidden_ref[...], grads_ref[...].reshape(3 * width // 2, length))
        part_out = [
            nn(out[...].reshape(width // 2, length), cot_ref[...])
            for out in (attended_a_ref, attended_b_ref)
        ]
        parts = jnp.concatenate([part_in, jnp.concatenate(part_out, axis=0)], axis=1)
        keep_and_send(core_ref[0], parts, keep_ref, send_ref)


def keep_and_send(core, parts, keep_ref, send_ref):
    half = parts.shape[1] // 2
    first, second = parts[:, :half], parts[:, half:]
    keep_ref[...] = jnp.where(core == 0, first, second)
    send_ref[...] = jnp.where(core == 0, second, first)


def backward_last_kernel(
    in_ref,
    gain_ref,
    probs_ref,
    hidden_ref,
    normed_ref,
    inverse_ref,
    query_x,
    key_x,
    values_ref,
    attended_ref,
    upstream_ref,
    first_ref,
    cot_ref,
    core_ref,
    *refs,
):
    grad_first, grad_second, keep_ref, send_ref, gain_out, grads = refs[-6:]
    step = pl.program_id(0)
    length, width = cot_ref.shape
    half = width // 2
    attend_back(
        probs_ref, query_x, key_x, values_ref, attended_ref, upstream_ref, grads, step
    )

    @pl.when(step == pl.num_programs(0) - 1)
    def _():
        grad_hidden = 0.0
        for group, ref in enumerate((first_ref, grads)):
            for part in range(3):
                first = part * width + group * half
                grad_hidden = grad_hidden + nn(
                    in_ref[:, first : first + half], ref[part].reshape(half, length)
                )
        parts = nt(hidden_ref[...], grads[...].reshape(3 * half, length))
        keep_and_send(core_ref[0], parts, keep_ref, send_ref)
        normed = normed_ref[...]
        part_gain = jnp.sum(grad_hidden * normed, axis=1, keepdims=True)
        part_gain = jnp.transpose(jnp.broadcast_to(part_gain, (width, LANES)))[:1, :]
        lines = [part_gain[:, start : start + LANES] for start in range(0, width, LANES)]
        lines.append(jnp.zeros((8 - len(lines), LANES), F32))
        gain_out[...] = jnp.concatenate(lines, axis=0)
        scaled = grad_hidden * gain_ref[:, :1].astype(F32)
        middle = jnp.mean(scaled, axis=0, keepdims=True)
        slope = jnp.mean(scaled * normed, axis=0, keepdims=True)
        change = inverse_ref[...] * (scaled - middle - normed * slope)
        grad = (cot_ref[...].astype(F32) + jnp.transpose(change)).astype(BF16)
        grad_first[...] = grad[: length // 2]
        grad_second[...] = grad[length // 2 :]


def backward_first(shift, pair, weights, probs, split, attended, hidden, core):
    half, width = pair[0].shape
    length = 2 * half
    head_width = width // HEADS
    some = HEADS // 2
    count = BACKWARD_HEADS
    group = (some, head_width, length)
    extended = (count, head_width + 16, length)
    return pl.pallas_call(
        backward_first_kernel,
        grid=(some // count,),
        in_specs=[
            SMEM,
            whole((half, width)),
            whole((half, width)),
            whole((half, width)),
            whole((half, width)),
            pl.BlockSpec((width, width), lambda h: (0, 3)),
            per_step((count, length, length), 0),
            per_step(extended, 0),
            per_step(extended, 0),
            per_step((count, head_width, length), 0),
            per_step((count, head_width, length), 0),
            whole((width, length)),
            whole(group),
            whole(group),
            SMEM,
        ],
        out_specs=[
            whole((length, width)),
            whole(group),
            whole((3,) + group),
            whole((width, 5 * width // 4)),
            whole((width, 5 * width // 4)),
        ],
        out_shape=[
            jax.ShapeDtypeStruct((length, width), BF16),
            jax.ShapeDtypeStruct(group, BF16),
            jax.ShapeDtypeStruct((3,) + group, BF16),
            jax.ShapeDtypeStruct((width, 5 * width // 4), F32),
            jax.ShapeDtypeStruct((width, 5 * width // 4), F32),
        ],
        scratch_shapes=[pltpu.VMEM(group, BF16)],
        compiler_params=params(),
        cost_estimate=lasting(25),
        name="backward_first",
    )(shift, *pair, weights, probs, *split, attended[0], hidden, *attended, core)


def backward_last(weights, probs, rows, split, attended, upstream, first, cot, core, after):
    length, width = cot.shape
    head_width = width // HEADS
    some = HEADS // 2
    count = BACKWARD_HEADS
    skip = some // count
    group = (some, head_width, length)
    extended = (count, head_width + 16, length)
    one = (count, head_width, length)
    return pl.pallas_call(
        backward_last_kernel,
        grid=(some // count,),
        in_specs=[
            pl.BlockSpec((width, 3 * width), lambda h: (0, 0)),
            pl.BlockSpec((width, GAIN_COLS), lambda h: (0, 4 * width // GAIN_COLS)),
            per_step((count, length, length), 0),
            whole((width, length)),
            whole((width, length)),
            whole((1, length)),
            per_step(extended, skip),
            per_step(extended, skip),
            per_step(one, skip),
            per_step(one, 0),
            per_step(one, 0),
            whole((3,) + group),
            whole((length, width)),
            SMEM,
        ]
        + [ANY] * len(after),
        out_specs=[
            whole((length // 2, width)),
            whole((length // 2, width)),
            whole((width, 3 * width // 4)),
            whole((width, 3 * width // 4)),
            whole((8, LANES)),
        ],
        out_shape=[
            jax.ShapeDtypeStruct((length // 2, width), BF16),
            jax.ShapeDtypeStruct((length // 2, width), BF16),
            jax.ShapeDtypeStruct((width, 3 * width // 4), F32),
            jax.ShapeDtypeStruct((width, 3 * width // 4), F32),
            jax.ShapeDtypeStruct((8, LANES), F32),
        ],
        scratch_shapes=[pltpu.VMEM((3,) + group, BF16)],
        compiler_params=params(),
        cost_estimate=lasting(25),
        name="backward_last",
    )(
        weights,
        weights,
        probs,
        *rows,
        *split,
        attended[1],
        upstream,
        first,
        cot,
        core,
        *after,
    )


def exchange(rows, devices):
    moved = lax.all_to_all(
        rows.reshape(devices, rows.shape[0] // devices, rows.shape[1]),
        BOTH,
        split_axis=0,
        concat_axis=0,
        tiled=True,
    )
    return moved.reshape(rows.shape)


def with_neighbours(first, second):
    devices = lax.axis_size(BOTH)
    ahead = [(seat(i), seat((i + 1) % devices)) for i in range(devices)]
    behind = [(j, i) for i, j in ahead]
    return first, second, lax.ppermute(first, BOTH, ahead), lax.ppermute(second, BOTH, behind)


def with_neighbours_back(first, second):
    devices = lax.axis_size(BOTH)
    ahead = [(seat(i), seat((i + 1) % devices)) for i in range(devices)]
    behind = [(j, i) for i, j in ahead]
    return first, second, lax.ppermute(first, BOTH, behind), lax.ppermute(second, BOTH, ahead)


def other_core(array):
    pairs = [(i, i ^ 1) for i in range(lax.axis_size("fsdp"))]
    return lax.ppermute(array, "fsdp", pairs)


def over_chips(terms):
    count, far = lax.axis_size("fsdp"), 2
    while far < count:
        terms = terms + lax.ppermute(terms, "fsdp", [(i, i ^ far) for i in range(count)])
        far *= 2
    return terms


def curve_work(shift_offset, got_points, send_cot, weights):
    devices, groups = lax.axis_size(BOTH), lax.axis_size("dp")
    width, share = send_cot.shape[1], weights.shape[0] // lax.axis_size("fsdp")
    edge_device = jnp.where(2 * shift_offset <= PATCH, seat(devices - 1), seat(0))
    wrap = (lax.axis_index(BOTH) == edge_device).astype(jnp.int32)
    core = (lax.axis_index("fsdp") % 2).astype(jnp.int32).reshape(1)

    *own_points, place = land_first(shift_offset, got_points, width, (send_cot,))
    points_pair = with_neighbours(*own_points)
    turned = turn(weights, width, (place,))
    got_cot = exchange(gate(send_cot, turned), devices)
    block, (probs_a, probs_b), split, attended, (hidden, normed, inverse) = forward(
        shift_offset, wrap, points_pair, weights, turned
    )
    cot_pair = with_neighbours(*land_second(place, got_cot, (probs_a,)))
    block_pair = with_neighbours_back(*block)

    cot, upstream, first_grads, first_keep, first_send = backward_first(
        shift_offset, cot_pair, weights, probs_a, split, attended, hidden, core
    )
    spread_block = spread_pair(shift_offset, place, block_pair, "back_block", after=(first_grads,))
    back_block = exchange(spread_block, devices)
    *grad, last_keep, last_send, part_gain = backward_last(
        weights,
        probs_b,
        (hidden, normed, inverse),
        split,
        attended,
        upstream,
        first_grads,
        cot,
        core,
        (spread_block,),
    )
    grad_pair = with_neighbours_back(*grad)
    parts = (first_keep, other_core(first_send), last_keep, other_core(last_send))
    gain_terms = over_chips(part_gain)
    spread_grad = spread_pair(
        shift_offset, place, grad_pair, "back_grad", parts, (groups, share), (back_block, gain_terms)
    )
    return spread_grad, back_block, gain_terms + other_core(gain_terms)


def body(
    points,
    cotangent,
    destination,
    curve_slot,
    point_counts,
    shift_offset,
    project_in,
    project_out,
    norm_gain,
):
    devices, groups = lax.axis_size(BOTH), lax.axis_size("dp")
    arrived, width = points.shape
    share = project_in.shape[0]
    packed = pack(project_in, project_out, norm_gain)
    weights = lax.all_gather(packed, "fsdp", axis=0, tiled=True)
    send_points, target = send_first(
        shift_offset,
        point_counts,
        destination.reshape(1, arrived),
        curve_slot.reshape(1, arrived),
        points,
        devices,
        (packed,),
    )
    got_points = exchange(send_points, devices)
    send_cot = pick(target, cotangent, arrived, "send_cot")
    spread_grad, back_block, gain_terms = curve_work(shift_offset, got_points, send_cot, weights)
    back_grad = exchange(spread_grad, devices)
    block_out = spread(target, back_block, width, "block_out", (spread_grad,))
    sums = add_tiles(back_grad, gain_terms, width, groups, (block_out,))
    tiles = lax.all_to_all(sums, "dp", split_axis=0, concat_axis=0, tiled=True)
    point_grad = spread(target, back_grad, width, "point_grad", (sums,))
    columns = (5 * width // 4, 3 * width // 4)
    member = lax.axis_index("fsdp").astype(jnp.int32).reshape(1)
    grad_in, grad_out, grad_gain = settle(member, tiles, (groups, share), columns, width)
    return block_out, point_grad, grad_in, grad_out, grad_gain.reshape(share)


def solution(mesh):
    in_specs = (
        P(BOTH, None),
        P(BOTH, None),
        P(BOTH),
        P(BOTH),
        P(BOTH),
        P(),
        P("fsdp", None),
        P("fsdp", None),
        P("fsdp"),
    )
    out_specs = (
        P(BOTH, None),
        P(BOTH, None),
        P("fsdp", None),
        P("fsdp", None),
        P("fsdp"),
    )
    return jax.shard_map(body, mesh=mesh, in_specs=in_specs, out_specs=out_specs, check_vma=False)
```
